32 devices in a mesh: row: 4 (over z), col: 8 (over y, x, core).
Axes of the slice: x: 2, y: 2, z: 4, core: 2. Of those that a mesh axis runs over, the one named last changes fastest.
Arguments:
- factor_inverse: bfloat16 [2048, 2048], P(('row', 'col')), as said below
- panel_left: float32 [16384, 256], P(('row', 'col')), may hold values from -6 to 6
- panel_right: float32 [16384, 256], P(('row', 'col')), may hold values from -12 to 12
- panel_rank: int32 [8], P('row'), may hold values from 16 to 256, as said below
- left: float32 [16384, 2048], P('row', 'col'), may hold values from -6 to 6
- right: float32 [16384, 2048], P('row', 'col'), may hold values from -6 to 6
- probes: float32 [16384, 2048], P('row', 'col'), may hold values from -6 to 6
- trail_rank: int32 [8, 8], P('row', 'col'), may hold values from 16 to 256, as said below
Outputs:
- new_left: float32 [16384, 2048], P('row', 'col')
- new_right: float32 [16384, 2048], P('row', 'col')
The draws below stay inside these ranges and needn't reach their ends.
Inputs may be any that keep to these rules, and one draw needn't show every extreme that they name: `factor_inverse`: lower triangular with a positive diagonal. `panel_rank`: every rank is a multiple of 16, and some panel tile has rank 256. `trail_rank`: every rank is a multiple of 16, and some trailing tile has rank 256.
All inputs are finite; a program needn't handle non-finite values.
Results may differ from the reference program's by a relative error of at most 0.0012.
Values may be sent and summed in bfloat16 or wider, within the bound.
No kernel may reach another device: no remote copies, remote signals or barrier semaphores. Data moves between devices by JAX's collectives and lax.ppermute only.
A program may use at most 128 MiB of HBM per device.

```python
import math
import jax
import jax.numpy as jnp
from jax import lax

NB = 2048
KMAX = 256
MT = 8


def rank_table(key, entries):
    first, second = jax.random.split(key)
    values = 16 * jax.random.randint(first, (entries,), 1, KMAX // 16 + 1)
    chosen = jax.random.randint(second, (), 0, entries)
    return jnp.where(jnp.arange(entries) == chosen, KMAX, values).astype(jnp.int32)


def draw_panel_rank(key, part):
    key = jax.random.fold_in(key, 5)
    return rank_table(key, MT)


def draw_trail_rank(key, part):
    key = jax.random.fold_in(key, 7)
    return rank_table(key, MT * MT).reshape(MT, MT)


def draw_factor_inverse(key, part):
    key = jax.random.fold_in(key, 11)
    first, second = jax.random.split(key)
    raw_values = jax.random.normal(first, (NB, NB), jnp.float32) * (0.6 / jnp.sqrt(NB * 1.0))
    diag_level = jax.random.uniform(second, (NB,), jnp.float32, 0.5, 1.0)
    positions = jnp.arange(NB)
    below = positions[:, None] > positions[None, :]
    on_diag = positions[:, None] == positions[None, :]
    result = jnp.where(below, raw_values, 0.0)
    return jnp.where(on_diag, diag_level[:, None], result).astype(jnp.bfloat16)


def level_of(key, dims, shards, smallest, largest):
    factor_of, own = 1.0, jax.random.fold_in(key, 6)
    for axis_at, blocks in shards:
        heights = jnp.exp(jax.random.uniform(jax.random.fold_in(own, axis_at), (blocks,), jnp.float32, smallest / len(shards), largest / len(shards)))
        factor_of = factor_of * jnp.repeat(heights, dims[axis_at] // blocks).reshape([-1 if axis == axis_at else 1 for axis in range(len(dims))])
    return factor_of


def noise(own_key, extent, spread, reach, shards=(), held_as=jnp.bfloat16):
    values = jax.random.normal(own_key, extent, jnp.float32) * spread
    if len(shards) > 0:
        values = level_of(own_key, extent, shards, -0.22, 0.18) * values
    return jnp.clip(values, min=-reach, max=reach).astype(held_as)


def setup_inputs(seed: int = 0) -> dict:
    streams_of = jax.random.split(jax.random.key(seed), 9)
    factor_inverse = draw_factor_inverse(jax.random.fold_in(streams_of[8], 71), 0)
    panel_left = noise(streams_of[1], (MT * NB, KMAX), 1.0, 6.0, ((0, 32),), jnp.float32)
    panel_right = noise(streams_of[2], (MT * NB, KMAX), 2.0, 12.0, ((0, 32),), jnp.float32)
    panel_rank = draw_panel_rank(jax.random.fold_in(streams_of[8], 71), 0)
    left = noise(streams_of[4], (MT * NB, MT * KMAX), 1.0, 6.0, ((0, 4), (1, 8)), jnp.float32)
    right = noise(streams_of[5], (MT * NB, MT * KMAX), 1.0, 6.0, ((0, 4), (1, 8)), jnp.float32)
    probes = noise(streams_of[6], (MT * NB, MT * KMAX), 1.0, 6.0, ((0, 4), (1, 8)), jnp.float32)
    trail_rank = draw_trail_rank(jax.random.fold_in(streams_of[8], 71), 0)
    return dict(factor_inverse=factor_inverse, panel_left=panel_left, panel_right=panel_right, panel_rank=panel_rank, left=left, right=right, probes=probes, trail_rank=trail_rank)


highest = lax.Precision.HIGHEST

def reference(factor_inverse, panel_left, panel_right, panel_rank, left, right, probes, trail_rank):
    inverse_lower = factor_inverse.astype(jnp.float32)
    columns = jnp.arange(KMAX, dtype=jnp.int32)
    panel_kept = (columns[None, :] < panel_rank[:, None]).astype(jnp.float32)
    masked_left = panel_left.reshape(MT, NB, KMAX) * panel_kept[:, None, :]
    masked_right = panel_right.reshape(MT, NB, KMAX) * panel_kept[:, None, :]
    stacked = masked_right.transpose(1, 0, 2).reshape(NB, MT * KMAX)
    solved_all = jnp.dot(inverse_lower, stacked, precision=highest)
    panel_solved = solved_all.reshape(NB, MT, KMAX).transpose(1, 0, 2)
    root_width = math.sqrt(NB)
    identity = (columns[:, None] == columns[None, :]).astype(jnp.float32)

    def update_row(row_items):
        left_row, right_row, probe_row, rank_row, row_left, row_solved = row_items
        kept_cols = (columns[None, :] < rank_row[:, None]).astype(jnp.float32)

        def to_tiles(block):
            return block.reshape(NB, MT, KMAX).transpose(1, 0, 2) * kept_cols[:, None, :]
        tile_left = to_tiles(left_row)
        tile_right = to_tiles(right_row)
        tile_probe = to_tiles(probe_row)
        panel_core = jnp.einsum('nk,qnl->qkl', row_solved, panel_solved, precision=highest) / NB
        right_probe = jnp.einsum('qnk,qnl->qkl', tile_right, tile_probe, precision=highest)
        panel_probe = jnp.einsum('qnk,qnl->qkl', masked_left, tile_probe, precision=highest)
        core_probe = jnp.einsum('qkl,qlm->qkm', panel_core, panel_probe, precision=highest)
        sampled = (jnp.einsum('qnk,qkl->qnl', tile_left, right_probe, precision=highest) - jnp.einsum('nk,qkl->qnl', row_left, core_probe, precision=highest)) / NB
        gram_matrix = jnp.einsum('qnk,qnl->qkl', sampled, sampled, precision=highest)
        gram_matrix = gram_matrix + (1.0 - kept_cols)[:, :, None] * identity
        gram_factor = jnp.linalg.cholesky(gram_matrix)
        new_basis = lax.linalg.triangular_solve(gram_factor, sampled, left_side=False, lower=True, transpose_a=True) * root_width
        left_proj = jnp.einsum('qnk,qnl->qkl', tile_left, new_basis, precision=highest)
        panel_proj = jnp.einsum('nk,qnl->qkl', row_left, new_basis, precision=highest)
        core_proj = jnp.einsum('qlk,qlm->qkm', panel_core, panel_proj, precision=highest)
        new_factor = (jnp.einsum('qnk,qkl->qnl', tile_right, left_proj, precision=highest) - jnp.einsum('qnk,qkl->qnl', masked_left, core_proj, precision=highest)) / NB
        return (new_basis.transpose(1, 0, 2).reshape(NB, MT * KMAX), new_factor.transpose(1, 0, 2).reshape(NB, MT * KMAX))
    out_left, out_right = lax.map(update_row, (left.reshape(MT, NB, MT * KMAX), right.reshape(MT, NB, MT * KMAX), probes.reshape(MT, NB, MT * KMAX), trail_rank, masked_left, panel_solved))
    return (out_left.reshape(MT * NB, MT * KMAX), out_right.reshape(MT * NB, MT * KMAX))
```

```python
import math

import jax
import jax.numpy as jnp
from jax import lax
from jax.sharding import PartitionSpec as P

highest = lax.Precision.HIGHEST


def flip(value, axis, size, mask):
    return lax.ppermute(value, axis, [(i, i ^ mask) for i in range(size)])


def dot(spec, a, b):
    return jnp.einsum(spec, a, b, precision=highest, preferred_element_type=jnp.float32)


def make_shards(rows, cols):
    pairs = cols // 2

    def shards(factor_inverse, panel_left, panel_right, panel_rank, left, right, probes, trail_rank):
        tile_rows, tile_cols = trail_rank.shape
        tile_order = factor_inverse.shape[1]
        rank_cap = left.shape[1] // tile_cols
        chunk = panel_left.shape[0]
        root_width = math.sqrt(tile_order)
        me = lax.axis_index("col")
        columns = jnp.arange(rank_cap, dtype=jnp.int32)
        my_pair, my_side = me // 2, me % 2

        def row_gather(block):
            held = [block] + [flip(block, "col", cols, 2 * d) for d in range(1, pairs)]
            other = flip(jnp.stack(held), "col", cols, 1)
            whole = jnp.zeros((cols,) + block.shape, block.dtype)
            for d in range(pairs):
                whole = lax.dynamic_update_index_in_dim(whole, held[d], me ^ (2 * d), 0)
                whole = lax.dynamic_update_index_in_dim(whole, other[d], me ^ (2 * d + 1), 0)
            return whole

        panel_kept = (columns[None, :] < panel_rank[:, None]).astype(jnp.float32)
        my_kept = lax.dynamic_index_in_dim(panel_kept, me // (cols // tile_rows), 0)
        masked_left = panel_left * my_kept
        masked_right = panel_right * my_kept

        inverse_rows = lax.all_gather(factor_inverse, "row", axis=0, tiled=True)
        row_right = row_gather(masked_right).reshape(tile_rows, tile_order, rank_cap)
        solved = jnp.concatenate(
            [dot("ij,jk->ik", inverse_rows.astype(jnp.float32), row_right[t]) for t in range(tile_rows)], axis=1
        )
        solved_all = lax.all_gather(solved, "row", axis=0)

        row_left = row_gather(masked_left).reshape(tile_rows, tile_order, rank_cap)

        slices = lax.all_gather(masked_left, "row", axis=0)
        got = [lax.dynamic_index_in_dim(slices, my_pair, 0, keepdims=False)]
        for d in range(1, pairs):
            out = lax.dynamic_index_in_dim(slices, my_pair ^ d, 0, keepdims=False)
            got.append(flip(out, "col", cols, 2 * d))
        got = jnp.stack(got).reshape(2, pairs // 2, chunk, rank_cap)
        top = my_pair // (pairs // 2)
        keep = lax.dynamic_index_in_dim(got, top ^ my_side, 0, keepdims=False)
        give = lax.dynamic_index_in_dim(got, top ^ my_side ^ 1, 0, keepdims=False)
        take = flip(give, "col", cols, 1)
        col_left = jnp.zeros((cols // 2, chunk, rank_cap), jnp.float32)
        low = my_pair % (pairs // 2)
        for d in range(pairs // 2):
            col_left = lax.dynamic_update_index_in_dim(col_left, keep[d], 2 * (low ^ d) + my_side, 0)
            col_left = lax.dynamic_update_index_in_dim(col_left, take[d], 2 * (low ^ d) + 1 - my_side, 0)
        col_left = col_left.reshape(tile_order, rank_cap)

        partial = dot("nk,rnl->rkl", solved, solved_all)
        partial = partial.reshape(rows, tile_rows, rank_cap, 2, rank_cap)
        partial = partial.transpose(3, 0, 1, 2, 4)
        mine = lax.dynamic_index_in_dim(partial, my_side, 0, keepdims=False)
        theirs = lax.dynamic_index_in_dim(partial, 1 - my_side, 0, keepdims=False)
        mine = mine + flip(theirs, "col", cols, 1)
        panel_core = lax.dynamic_index_in_dim(mine, my_pair, 0, keepdims=False)
        for d in range(1, pairs):
            out = lax.dynamic_index_in_dim(mine, my_pair ^ d, 0, keepdims=False)
            panel_core = panel_core + flip(out, "col", cols, 2 * d)
        panel_core = panel_core / tile_order

        kept_cols = (columns[None, :] < trail_rank).astype(jnp.float32)[:, None, :]

        def to_tiles(block):
            return block.reshape(tile_rows, tile_order, rank_cap) * kept_cols

        tile_left = to_tiles(left)
        tile_right = to_tiles(right)
        tile_probe = to_tiles(probes)
        right_probe = dot("tnk,tnl->tkl", tile_right, tile_probe)
        tile_part = dot("tnk,tkl->tnl", tile_left, right_probe)
        panel_probe = dot("nk,tnl->tkl", col_left, tile_probe)
        core_probe = dot("tkl,tlm->tkm", panel_core, panel_probe)
        sampled = (tile_part - dot("tnk,tkl->tnl", row_left, core_probe)) / tile_order
        identity = (columns[:, None] == columns[None, :]).astype(jnp.float32)
        gram_matrix = dot("tnk,tnl->tkl", sampled, sampled)
        gram_matrix = gram_matrix + (1.0 - kept_cols) * identity
        gram_factor = jnp.linalg.cholesky(gram_matrix)
        new_basis = (
            lax.linalg.triangular_solve(gram_factor, sampled, left_side=False, lower=True, transpose_a=True)
            * root_width
        )
        left_proj = dot("tnk,tnl->tkl", tile_left, new_basis)
        panel_proj = dot("tnk,tnl->tkl", row_left, new_basis)
        core_proj = dot("tlk,tlm->tkm", panel_core, panel_proj)
        new_factor = (
            dot("tnk,tkl->tnl", tile_right, left_proj) - dot("nk,tkl->tnl", col_left, core_proj)
        ) / tile_order
        return (
            new_basis.reshape(tile_rows * tile_order, rank_cap),
            new_factor.reshape(tile_rows * tile_order, rank_cap),
        )

    return shards


def solution(mesh):
    return jax.shard_map(
        make_shards(mesh.shape["row"], mesh.shape["col"]),
        mesh=mesh,
        in_specs=(
            P(("row", "col"), None),
            P(("row", "col"), None),
            P(("row", "col"), None),
            P("row"),
            P("row", "col"),
            P("row", "col"),
            P("row", "col"),
            P("row", "col"),
        ),
        out_specs=(P("row", "col"), P("row", "col")),
        check_vma=False,
    )
```

```python
import math

import jax
import jax.numpy as jnp
from jax import lax
from jax.experimental import pallas as pl
from jax.experimental.pallas import tpu as pltpu
from jax.sharding import PartitionSpec as P

highest = lax.Precision.HIGHEST
SUB = 8


def split_three(x):
    a = x.astype(jnp.bfloat16)
    r = x - a.astype(jnp.float32)
    b = r.astype(jnp.bfloat16)
    c = (r - b.astype(jnp.float32)).astype(jnp.bfloat16)
    return a, b, c


def hot_dot(x, y, dims):
    return lax.dot_general(x, y, (dims, ((), ())), precision=lax.Precision.HIGHEST, preferred_element_type=jnp.float32)


def factor_blocks(block, scratch):
    count = len(block)
    n = block[0].shape[0]
    wide = 2 * n
    groups = n // SUB
    lane = lax.broadcasted_iota(jnp.int32, (SUB, wide), 1)
    sub = lax.broadcasted_iota(jnp.int32, (SUB, wide), 0)
    state = []
    for t in range(count):
        eye = [jnp.where(lane - n == sub + SUB * g, 1.0, 0.0) for g in range(groups)]
        full = jnp.concatenate([block[t], jnp.zeros((n, n), jnp.float32)], axis=1)
        state.append([full[SUB * g : SUB * (g + 1)] + eye[g] for g in range(groups)])
    out = [[None] * groups for _ in range(count)]
    for k in range(groups):
        for t in range(count):
            rows = state[t]
            spread = [
                [jnp.broadcast_to(rows[g][:, SUB * k + j : SUB * k + j + 1], (SUB, wide)) for j in range(SUB)]
                for g in range(k, groups)
            ]
            for j in range(SUB):
                scratch[t, j] = spread[0][j]
            scratch[t, SUB] = rows[k]
            a = [
                [jnp.broadcast_to(scratch[t, j, i : i + 1, :], (SUB, wide)) for j in range(i + 1)]
                for i in range(SUB)
            ]
            row = [jnp.broadcast_to(scratch[t, SUB, i : i + 1, :], (SUB, wide)) for i in range(SUB)]
            inv = [None] * SUB
            low = [[None] * SUB for _ in range(SUB)]
            for j in range(SUB):
                inv[j] = 1.0 / a[j][j]
                for i in range(j + 1, SUB):
                    low[i][j] = a[i][j] * inv[j]
                for i in range(j + 1, SUB):
                    for h in range(i, SUB):
                        a[h][i] = a[h][i] - low[h][j] * a[i][j]
                    row[i] = row[i] - low[i][j] * row[j]
            done = row[0] * lax.rsqrt(a[0][0])
            for i in range(1, SUB):
                done = jnp.where(sub == i, row[i] * lax.rsqrt(a[i][i]), done)
            out[t][k] = done
            for g in range(k + 1, groups):
                cols = spread[g - k]
                scaled = []
                value = rows[g]
                for j in range(SUB):
                    x = cols[j]
                    for h in range(j):
                        x = x - scaled[h] * a[j][h]
                    scaled.append(x * inv[j])
                    value = value - scaled[j] * row[j]
                rows[g] = value
    return [jnp.concatenate(o, axis=0)[:, n:] for o in out]


def inverse_factor(gram_of, put, order, step, scratch, count):
    work = [gram_of(t) for t in range(count)]
    eye = (
        lax.broadcasted_iota(jnp.int32, (order, order), 0) == lax.broadcasted_iota(jnp.int32, (order, order), 1)
    )
    scale = []
    for t in range(count):
        diag = jnp.where(eye, work[t], 0.0)
        down = lax.rsqrt(jnp.sum(diag, axis=1, keepdims=True))
        across = lax.rsqrt(jnp.sum(diag, axis=0, keepdims=True))
        scale.append(across)
        work[t] = jnp.concatenate([work[t] * down * across, jnp.where(eye, 1.0, 0.0)], axis=1)
    for k in range(order // step):
        lo = k * step
        inner = factor_blocks([w[:step, lo : lo + step] for w in work], scratch)
        for t in range(count):
            solved = hot_dot(inner[t], work[t][:step], ((1,), (0,)))
            put(t, lo, solved[:, order:] * scale[t])
            if lo + step < order:
                tail = solved[:, lo + step : order]
                work[t] = work[t][step:] - hot_dot(tail, solved, ((0,), (0,)))


def factor_kernel(gram_ref, out_ref, scratch):
    count, order, _ = gram_ref.shape

    def put(t, lo, value):
        out_ref[t, lo : lo + value.shape[0], :] = value

    inverse_factor(lambda t: gram_ref[t], put, order, 64, scratch, count)


def factor(gram, **kw):
    return pl.pallas_call(
        factor_kernel,
        out_shape=jax.ShapeDtypeStruct(gram.shape, jnp.float32),
        in_specs=[pl.BlockSpec(memory_space=pltpu.VMEM)],
        out_specs=pl.BlockSpec(memory_space=pltpu.VMEM),
        scratch_shapes=[pltpu.VMEM((gram.shape[0], SUB + 1, SUB, 128), jnp.float32)],
        compiler_params=pltpu.CompilerParams(vmem_limit_bytes=32 * 1024 * 1024),
        **kw,
    )(gram)


def flip(value, axis, size, mask):
    return lax.ppermute(value, axis, [(i, i ^ mask) for i in range(size)])


def dot(spec, a, b):
    return jnp.einsum(spec, a, b, precision=highest, preferred_element_type=jnp.float32)


def call(kernel, out, args, kinds, scratch=(), limit=40):
    spaces = {"v": pltpu.VMEM, "s": pltpu.SMEM, "a": pl.ANY}
    flat = jax.tree.leaves(out)
    shapes = [jax.ShapeDtypeStruct(s.shape, s.dtype) for s in flat]
    where = pl.ANY if kinds[-1] == "a" else pltpu.VMEM
    result = pl.pallas_call(
        kernel,
        out_shape=shapes,
        in_specs=[pl.BlockSpec(memory_space=spaces[k]) for k in kinds[:-1]],
        out_specs=[pl.BlockSpec(memory_space=where)] * len(shapes),
        scratch_shapes=list(scratch),
        compiler_params=pltpu.CompilerParams(vmem_limit_bytes=limit * 1024 * 1024),
    )(*args)
    return result


def shaped(shape, dtype=jnp.float32):
    return jax.ShapeDtypeStruct(shape, dtype)


def solve_kernel(rows, pairs, where_ref, rank_ref, *refs):
    inverse, held, other = refs[:rows], refs[rows : rows + pairs], refs[rows + pairs]
    out_ref, whole = refs[rows + pairs + 1 :]
    floor, me = where_ref[0], where_ref[1]
    part = inverse[0].shape[0]
    chunk, cap = held[0].shape
    quarters = pairs
    half, quarter = me // quarters, me % quarters
    for d in range(rows):
        whole[pl.ds(pl.multiple_of((floor ^ d) * part, part), part), :] = inverse[d][...]
    column = lax.broadcasted_iota(jnp.int32, (1, cap), 1)
    for h in range(2):
        total = None
        for d in range(quarters):
            at = h * quarters + d
            value = held[at // 2][...] if at % 2 == 0 else other[at // 2]
            lhs = whole[:, pl.ds(pl.multiple_of((quarter ^ d) * chunk, chunk), chunk)]
            for piece in split_three(value):
                term = jnp.dot(lhs, piece, preferred_element_type=jnp.float32)
                total = term if total is None else total + term
        tile = half ^ h
        kept = column < rank_ref[tile]
        out_ref[:, pl.ds(pl.multiple_of(tile * cap, cap), cap)] = jnp.where(kept, total, 0.0)


def core_kernel(rows, pairs, where_ref, *refs):
    solved, (mine_ref, theirs_ref) = refs[:rows], refs[rows:]
    floor, me = where_ref[0], where_ref[1]
    pair, side = me // 2, me % 2
    cap = mine_ref.shape[2]
    own = solved[0][...]
    own_high = own.astype(jnp.bfloat16)
    own_low = (own - own_high.astype(jnp.float32)).astype(jnp.bfloat16)

    def across(x, y):
        return lax.dot_general(x, y, (((0,), (0,)), ((), ())), preferred_element_type=jnp.float32)

    for e in range(pairs):
        wanted = floor ^ pair ^ e
        value = own
        for d in range(1, rows):
            value = jnp.where(wanted == d, solved[d][...], value)
        high = value.astype(jnp.bfloat16)
        low = (value - high.astype(jnp.float32)).astype(jnp.bfloat16)
        part = across(own_high, high) + (across(own_high, low) + across(own_low, high))
        left, right = part[:, :cap], part[:, cap:]
        mine_ref[e] = jnp.where(side == 0, left, right)
        theirs_ref[e] = jnp.where(side == 0, right, left)


def place_kernel(count, slot_ref, *refs):
    blocks, out_ref, sem = refs[: -2], refs[-2], refs[-1]
    flat = []
    for b in blocks:
        flat += [b] if len(b.shape) == 2 else [b.at[i] for i in range(b.shape[0])]
    copies = []
    for n in range(count):
        chunk = flat[n].shape[0]
        at = pl.multiple_of(slot_ref[n] * chunk, chunk)
        copies.append(pltpu.make_async_copy(flat[n], out_ref.at[pl.ds(at, chunk)], sem.at[n]))
    for c in copies:
        c.start()
    for c in copies:
        c.wait()


def place(slots, blocks, count):
    chunk, width = blocks[0].shape[-2:]
    return call(
        lambda *refs: place_kernel(count, *refs),
        [shaped((count * chunk, width))],
        [jnp.stack(slots), *blocks],
        "s" + "a" * (len(blocks) + 1),
        [pltpu.SemaphoreType.DMA((count,))],
    )[0]


def make_shards(rows, cols):
    pairs = cols // 2

    def shards(factor_inverse, panel_left, panel_right, panel_rank, left, right, probes, trail_rank):
        tile_rows, tile_cols = trail_rank.shape
        tile_order = factor_inverse.shape[1]
        rank_cap = left.shape[1] // tile_cols
        chunk = panel_left.shape[0]
        part = factor_inverse.shape[0]
        root_width = math.sqrt(tile_order)
        me = lax.axis_index("col").astype(jnp.int32)
        floor = lax.axis_index("row").astype(jnp.int32)
        spot = jnp.stack([floor, me])
        columns = jnp.arange(rank_cap, dtype=jnp.int32)
        my_pair, my_side = me // 2, me % 2

        def row_gather(block):
            held = [block] + [flip(block, "col", cols, 2 * d) for d in range(1, pairs)]
            return held, flip(jnp.stack(held), "col", cols, 1)

        inverse = [factor_inverse] + [flip(factor_inverse, "row", rows, d) for d in range(1, rows)]
        slices = lax.all_gather(panel_left, "row", axis=0)
        held, other = row_gather(panel_right)
        solved = call(
            lambda *refs: solve_kernel(rows, pairs, *refs),
            [shaped((rows * part, tile_rows * rank_cap))],
            [spot, panel_rank, *inverse, *held, other],
            "ss" + "v" * (rows + pairs + 2),
            [pltpu.VMEM((rows * part, tile_order), jnp.bfloat16)],
        )[0]
        all_solved = [solved] + [flip(solved, "row", rows, d) for d in range(1, rows)]

        held, other = row_gather(panel_left)
        row_left = place([me ^ (2 * d) for d in range(pairs)] + [me ^ (2 * d + 1) for d in range(pairs)], [*held, other], cols)
        row_left = row_left.reshape(tile_rows, tile_order, rank_cap)

        got = [lax.dynamic_index_in_dim(slices, my_pair ^ d, 0, keepdims=False) for d in range(pairs)]
        got = [flip(got[d], "col", cols, 2 * d) if d else got[d] for d in range(pairs)]
        half = pairs // 2
        top = my_pair // half
        upper = (top ^ my_side) == 1
        keep = [jnp.where(upper, got[half + d], got[d]) for d in range(half)]
        give = [jnp.where(upper, got[d], got[half + d]) for d in range(half)]
        take = flip(jnp.stack(give), "col", cols, 1)
        low = my_pair % half
        col_left = place(
            [2 * (low ^ d) + my_side for d in range(half)] + [2 * (low ^ d) + 1 - my_side for d in range(half)],
            [*keep, take],
            pairs,
        )

        mine, theirs = call(
            lambda *refs: core_kernel(rows, pairs, *refs),
            [shaped((pairs, tile_rows * rank_cap, rank_cap))] * 2,
            [spot, *all_solved],
            "s" + "v" * (rows + 1),
        )
        theirs = flip(theirs, "col", cols, 1)
        parts = [mine[e] + theirs[e] for e in range(pairs)]
        panel_core = sum(flip(parts[e], "col", cols, 2 * e) if e else parts[e] for e in range(pairs))
        panel_core = panel_core.reshape(tile_rows, rank_cap, rank_cap) / tile_order

        kept_cols = (columns[None, :] < trail_rank).astype(jnp.float32)[:, None, :]

        def to_tiles(block):
            return block.reshape(tile_rows, tile_order, rank_cap) * kept_cols

        tile_left = to_tiles(left)
        tile_right = to_tiles(right)
        tile_probe = to_tiles(probes)
        right_probe = dot("tnk,tnl->tkl", tile_right, tile_probe)
        tile_part = dot("tnk,tkl->tnl", tile_left, right_probe)
        panel_probe = dot("nk,tnl->tkl", col_left, tile_probe)
        core_probe = dot("tkl,tlm->tkm", panel_core, panel_probe)
        sampled = (tile_part - dot("tnk,tkl->tnl", row_left, core_probe)) / tile_order
        identity = (columns[:, None] == columns[None, :]).astype(jnp.float32)
        gram_matrix = dot("tnk,tnl->tkl", sampled, sampled)
        gram_matrix = gram_matrix + (1.0 - kept_cols) * identity
        inverse_gram = factor(gram_matrix)
        new_basis = dot("tnk,tlk->tnl", sampled, inverse_gram) * root_width
        left_proj = dot("tnk,tnl->tkl", tile_left, new_basis)
        panel_proj = dot("tnk,tnl->tkl", row_left, new_basis)
        core_proj = dot("tlk,tlm->tkm", panel_core, panel_proj)
        new_factor = (
            dot("tnk,tkl->tnl", tile_right, left_proj) - dot("nk,tkl->tnl", col_left, core_proj)
        ) / tile_order
        return (
            new_basis.reshape(tile_rows * tile_order, rank_cap),
            new_factor.reshape(tile_rows * tile_order, rank_cap),
        )

    return shards


def solution(mesh):
    return jax.shard_map(
        make_shards(mesh.shape["row"], mesh.shape["col"]),
        mesh=mesh,
        in_specs=(
            P(("row", "col"), None),
            P(("row", "col"), None),
            P(("row", "col"), None),
            P("row"),
            P("row", "col"),
            P("row", "col"),
            P("row", "col"),
            P("row", "col"),
        ),
        out_specs=(P("row", "col"), P("row", "col")),
        check_vma=False,
    )
```

```python
import math

import jax
import jax.numpy as jnp
from jax import lax
from jax.experimental import pallas as pl
from jax.experimental.pallas import tpu as pltpu
from jax.sharding import PartitionSpec as P

highest = lax.Precision.HIGHEST
SUB = 8


def split_three(x):
    a = x.astype(jnp.bfloat16)
    r = x - a.astype(jnp.float32)
    b = r.astype(jnp.bfloat16)
    c = (r - b.astype(jnp.float32)).astype(jnp.bfloat16)
    return a, b, c


def hot_dot(x, y, dims):
    return lax.dot_general(x, y, (dims, ((), ())), precision=lax.Precision.HIGHEST, preferred_element_type=jnp.float32)


def factor_blocks(block, scratch):
    count = len(block)
    n = block[0].shape[0]
    wide = 2 * n
    groups = n // SUB
    lane = lax.broadcasted_iota(jnp.int32, (SUB, wide), 1)
    sub = lax.broadcasted_iota(jnp.int32, (SUB, wide), 0)
    state = []
    for t in range(count):
        eye = [jnp.where(lane - n == sub + SUB * g, 1.0, 0.0) for g in range(groups)]
        full = jnp.concatenate([block[t], jnp.zeros((n, n), jnp.float32)], axis=1)
        state.append([full[SUB * g : SUB * (g + 1)] + eye[g] for g in range(groups)])
    out = [[None] * groups for _ in range(count)]
    for k in range(groups):
        for t in range(count):
            rows = state[t]
            spread = [
                [jnp.broadcast_to(rows[g][:, SUB * k + j : SUB * k + j + 1], (SUB, wide)) for j in range(SUB)]
                for g in range(k, groups)
            ]
            for j in range(SUB):
                scratch[t, j] = spread[0][j]
            scratch[t, SUB] = rows[k]
            a = [
                [jnp.broadcast_to(scratch[t, j, i : i + 1, :], (SUB, wide)) for j in range(i + 1)]
                for i in range(SUB)
            ]
            row = [jnp.broadcast_to(scratch[t, SUB, i : i + 1, :], (SUB, wide)) for i in range(SUB)]
            inv = [None] * SUB
            low = [[None] * SUB for _ in range(SUB)]
            for j in range(SUB):
                inv[j] = 1.0 / a[j][j]
                for i in range(j + 1, SUB):
                    low[i][j] = a[i][j] * inv[j]
                for i in range(j + 1, SUB):
                    for h in range(i, SUB):
                        a[h][i] = a[h][i] - low[h][j] * a[i][j]
                    row[i] = row[i] - low[i][j] * row[j]
            done = row[0] * lax.rsqrt(a[0][0])
            for i in range(1, SUB):
                done = jnp.where(sub == i, row[i] * lax.rsqrt(a[i][i]), done)
            out[t][k] = done
            for g in range(k + 1, groups):
                cols = spread[g - k]
                scaled = []
                value = rows[g]
                for j in range(SUB):
                    x = cols[j]
                    for h in range(j):
                        x = x - scaled[h] * a[j][h]
                    scaled.append(x * inv[j])
                    value = value - scaled[j] * row[j]
                rows[g] = value
    return [jnp.concatenate(o, axis=0)[:, n:] for o in out]


def inverse_factor(gram_of, put, order, step, scratch, count):
    work = [gram_of(t) for t in range(count)]
    eye = (
        lax.broadcasted_iota(jnp.int32, (order, order), 0) == lax.broadcasted_iota(jnp.int32, (order, order), 1)
    )
    scale = []
    for t in range(count):
        diag = jnp.where(eye, work[t], 0.0)
        down = lax.rsqrt(jnp.sum(diag, axis=1, keepdims=True))
        across = lax.rsqrt(jnp.sum(diag, axis=0, keepdims=True))
        scale.append(across)
        work[t] = jnp.concatenate([work[t] * down * across, jnp.where(eye, 1.0, 0.0)], axis=1)
    for k in range(order // step):
        lo = k * step
        inner = factor_blocks([w[:step, lo : lo + step] for w in work], scratch)
        for t in range(count):
            solved = hot_dot(inner[t], work[t][:step], ((1,), (0,)))
            put(t, lo, solved[:, order:] * scale[t])
            if lo + step < order:
                tail = solved[:, lo + step : order]
                work[t] = work[t][step:] - hot_dot(tail, solved, ((0,), (0,)))


def factor_kernel(gram_ref, out_ref, scratch):
    count, order, _ = gram_ref.shape

    def put(t, lo, value):
        out_ref[t, lo : lo + value.shape[0], :] = value

    inverse_factor(lambda t: gram_ref[t], put, order, 64, scratch, count)


def factor(gram, **kw):
    return pl.pallas_call(
        factor_kernel,
        out_shape=jax.ShapeDtypeStruct(gram.shape, jnp.float32),
        in_specs=[pl.BlockSpec(memory_space=pltpu.VMEM)],
        out_specs=pl.BlockSpec(memory_space=pltpu.VMEM),
        scratch_shapes=[pltpu.VMEM((gram.shape[0], SUB + 1, SUB, 128), jnp.float32)],
        compiler_params=pltpu.CompilerParams(vmem_limit_bytes=32 * 1024 * 1024),
        **kw,
    )(gram)


def flip(value, axis, size, mask):
    return lax.ppermute(value, axis, [(i, i ^ mask) for i in range(size)])


def after(value, *earlier):
    return lax.optimization_barrier((value, *earlier))[0]


def dot(spec, a, b):
    return jnp.einsum(spec, a, b, precision=highest, preferred_element_type=jnp.float32)


def shaped(shape, dtype=jnp.float32):
    return jax.ShapeDtypeStruct(shape, dtype)


def call(kernel, out, args, kinds, scratch=(), limit=48, flops=0):
    spaces = {"v": pltpu.VMEM, "s": pltpu.SMEM, "a": pl.ANY}
    moved = sum(a.size * a.dtype.itemsize for a in [*out, *args])
    return pl.pallas_call(
        kernel,
        out_shape=out,
        in_specs=[pl.BlockSpec(memory_space=spaces[k]) for k in kinds[: len(args)]],
        out_specs=[pl.BlockSpec(memory_space=spaces[k]) for k in kinds[len(args) :]],
        scratch_shapes=list(scratch),
        compiler_params=pltpu.CompilerParams(vmem_limit_bytes=limit * 1024 * 1024),
        cost_estimate=pl.CostEstimate(flops=flops, bytes_accessed=moved, transcendentals=0),
    )(*args)


def power_of_two(exponent):
    low = exponent + 128
    value = jnp.full(exponent.shape, 2.0**-64, jnp.float32)
    for bit in range(7):
        value = value * jnp.where((low >> bit) & 1 == 1, 2.0 ** (2**bit), 1.0)
    return value * jnp.where(low >= 128, 1.0, 2.0**-64) * jnp.where(low >= 128, 2.0**64, 1.0)


def packed_rows(rows):
    return rows // 4 * 3 + 8


def pack_into(value, out_ref):
    rows, width = value.shape
    piece = rows // 4
    top = jnp.max(jnp.abs(value), axis=0, keepdims=True)
    level = jnp.log(jnp.maximum(top, 2.0**-90)) * 1.4426950408889634
    exponent = jnp.floor(level).astype(jnp.int32) + 1
    factor_up = power_of_two(23 - exponent)
    limit = 2.0**23 - 1
    codes = [
        jnp.clip(jnp.round(value[piece * n : piece * (n + 1)] * factor_up), -limit, limit).astype(jnp.int32)
        for n in range(4)
    ]
    for n in range(3):
        out_ref[piece * n : piece * (n + 1), :] = (codes[n] << 8) | ((codes[3] >> (8 * n)) & 255)
    out_ref[3 * piece :, :] = jnp.broadcast_to(exponent, (8, width))


def unpack(words):
    rows, width = words.shape
    piece = (rows - 8) // 3
    part = [words[piece * n : piece * (n + 1)] for n in range(3)]
    down = power_of_two(words[3 * piece : 3 * piece + 1] - 23)
    last = ((part[2] << 24) | ((part[1] & 255) << 16) | ((part[0] & 255) << 8)) >> 8
    codes = [p >> 8 for p in part] + [last]
    return [c.astype(jnp.float32) * down for c in codes]


def load_all(pairs_of, sem):
    copies = [pltpu.make_async_copy(src, dst, sem.at[n]) for n, (src, dst) in enumerate(pairs_of)]
    for c in copies:
        c.start()
    for c in copies:
        c.wait()


def pack_kernel(value_ref, out_ref):
    pack_into(value_ref[...], out_ref)


def solve_kernel(rows, pairs, where_ref, rank_ref, *refs):
    inverse, held, other = refs[:rows], refs[rows : rows + pairs], refs[rows + pairs]
    out_ref, packed_ref, whole, right, sem = refs[rows + pairs + 1 :]
    floor, me = where_ref[0], where_ref[1]
    part = inverse[0].shape[0]
    chunk, cap = held[0].shape
    quarters = pairs
    half, quarter = me // quarters, me % quarters
    moves = [
        (inverse[d], whole.at[pl.ds(pl.multiple_of((floor ^ d) * part, part), part), :]) for d in range(rows)
    ]
    for at in range(2 * pairs):
        moves.append((held[at // 2] if at % 2 == 0 else other.at[at // 2], right.at[at]))
    load_all(moves, sem)
    column = lax.broadcasted_iota(jnp.int32, (1, cap), 1)
    for h in range(2):
        total = None
        for d in range(quarters):
            lhs = whole[:, pl.ds(pl.multiple_of((quarter ^ d) * chunk, chunk), chunk)]
            for piece in split_three(right[h * quarters + d]):
                term = jnp.dot(lhs, piece, preferred_element_type=jnp.float32)
                total = term if total is None else total + term
        tile = half ^ h
        kept = column < rank_ref[tile]
        out_ref[:, pl.ds(pl.multiple_of(tile * cap, cap), cap)] = jnp.where(kept, total, 0.0)
    pack_into(out_ref[...], packed_ref)


def core_kernel(rows, pairs, where_ref, own_ref, *refs):
    arrived, (mine_ref, theirs_ref, solved, sem) = refs[: rows - 1], refs[rows - 1 :]
    floor, me = where_ref[0], where_ref[1]
    pair, side = me // 2, me % 2
    cap = mine_ref.shape[2]
    own = own_ref[...]
    load_all([(arrived[d], solved.at[d]) for d in range(rows - 1)], sem)

    def halves(x):
        high = x.astype(jnp.bfloat16)
        return high, (x - high.astype(jnp.float32)).astype(jnp.bfloat16)

    own_high, own_low = halves(own)

    def across(x, y):
        return lax.dot_general(x, y, (((0,), (0,)), ((), ())), preferred_element_type=jnp.float32)

    for e in range(pairs):
        wanted = floor ^ pair ^ e
        there = jnp.concatenate(unpack(solved[jnp.maximum(wanted, 1) - 1]), axis=0)
        high, low = halves(jnp.where(wanted == 0, own, there))
        part = across(own_high, high) + (across(own_high, low) + across(own_low, high))
        left, right = part[:, :cap], part[:, cap:]
        mine_ref[e] = jnp.where(side == 0, left, right)
        theirs_ref[e] = jnp.where(side == 0, right, left)


def choose_kernel(rows, pairs, where_ref, *refs):
    ins, outs, sem = refs[:rows], refs[rows : rows + pairs], refs[rows + pairs]
    mark = where_ref[0] ^ (where_ref[1] // 2)
    for g in range(rows):

        @pl.when(mark == g)
        def _(g=g):
            load_all([(ins[g ^ e], outs[e]) for e in range(pairs)], sem)


def spread_kernel(count, slot_ref, *refs):
    blocks, (out_ref, words, sem) = refs[:-3], refs[-3:]
    flat = []
    for b in blocks:
        flat += [b] if len(b.shape) == 2 else [b.at[i] for i in range(b.shape[0])]
    load_all([(flat[n], words.at[n]) for n in range(count)], sem)
    for n in range(count):
        values = unpack(words[n])
        piece = values[0].shape[0]
        for i in range(4):
            at = pl.multiple_of(slot_ref[n] * (4 * piece) + piece * i, piece)
            out_ref[pl.ds(at, piece), :] = values[i]


def spread(slots, blocks, count):
    words, width = blocks[0].shape[-2:]
    chunk = (words - 8) // 3 * 4
    return call(
        lambda *refs: spread_kernel(count, *refs),
        [shaped((count * chunk, width))],
        [jnp.stack(slots), *blocks],
        "s" + "a" * len(blocks) + "v",
        [pltpu.VMEM((count, words, width), jnp.int32), pltpu.SemaphoreType.DMA((count,))],
    )[0]


def make_shards(rows, cols):
    pairs = cols // 2

    def shards(factor_inverse, panel_left, panel_right, panel_rank, left, right, probes, trail_rank):
        tile_rows, tile_cols = trail_rank.shape
        tile_order = factor_inverse.shape[1]
        rank_cap = left.shape[1] // tile_cols
        chunk = panel_left.shape[0]
        part = factor_inverse.shape[0]
        root_width = math.sqrt(tile_order)
        me = lax.axis_index("col").astype(jnp.int32)
        floor = lax.axis_index("row").astype(jnp.int32)
        spot = jnp.stack([floor, me])
        columns = jnp.arange(rank_cap, dtype=jnp.int32)
        my_pair, my_side = me // 2, me % 2
        wide = tile_rows * rank_cap

        inverse = [factor_inverse] + [flip(factor_inverse, "row", rows, d) for d in range(1, rows)]
        held = [panel_right] + [flip(panel_right, "col", cols, 2 * d) for d in range(1, pairs)]
        other = flip(jnp.stack(held), "col", cols, 1)

        words = call(pack_kernel, [shaped((packed_rows(chunk), rank_cap), jnp.int32)], [panel_left], "vv")[0]
        words_z = after(words, *inverse[1:])
        from_floors = [words_z] + [flip(words_z, "row", rows, d) for d in range(1, rows)]
        words_p = after(words, *held[1:])
        row_held = [words_p] + [flip(words_p, "col", cols, 2 * d) for d in range(1, pairs)]

        solved, solved_words = call(
            lambda *refs: solve_kernel(rows, pairs, *refs),
            [shaped((rows * part, wide)), shaped((packed_rows(rows * part), wide), jnp.int32)],
            [spot, panel_rank, *inverse, *held, other],
            "ss" + "a" * (rows + pairs + 1) + "vv",
            [
                pltpu.VMEM((rows * part, tile_order), jnp.bfloat16),
                pltpu.VMEM((cols, chunk, rank_cap), jnp.float32),
                pltpu.SemaphoreType.DMA((rows + cols,)),
            ],
            flops=6 * rows * part * tile_order * wide,
        )
        arrived = [flip(solved_words, "row", rows, d) for d in range(1, rows)]

        row_other = flip(jnp.stack(row_held), "col", cols, 1)
        row_left = spread(
            [me ^ (2 * d) for d in range(pairs)] + [me ^ (2 * d + 1) for d in range(pairs)],
            [*row_held, row_other],
            cols,
        ).reshape(tile_rows, tile_order, rank_cap)

        got = call(
            lambda *refs: choose_kernel(rows, pairs, *refs),
            [shaped(words.shape, jnp.int32)] * pairs,
            [spot, *from_floors],
            "s" + "a" * (rows + pairs),
            [pltpu.SemaphoreType.DMA((pairs,))],
        )
        got = [flip(got[d], "col", cols, 2 * d) if d else got[d] for d in range(pairs)]
        half = pairs // 2
        top = my_pair // half
        upper = (top ^ my_side) == 1
        keep = [jnp.where(upper, got[half + d], got[d]) for d in range(half)]
        give = [jnp.where(upper, got[d], got[half + d]) for d in range(half)]
        take = flip(jnp.stack(give), "col", cols, 1)
        low = my_pair % half
        col_left = spread(
            [2 * (low ^ d) + my_side for d in range(half)] + [2 * (low ^ d) + 1 - my_side for d in range(half)],
            [*keep, take],
            pairs,
        )

        mine, theirs = call(
            lambda *refs: core_kernel(rows, pairs, *refs),
            [shaped((pairs, wide, rank_cap))] * 2,
            [spot, solved, *arrived],
            "sv" + "a" * (rows - 1) + "vv",
            [
                pltpu.VMEM((rows - 1, *solved_words.shape), jnp.int32),
                pltpu.SemaphoreType.DMA((rows - 1,)),
            ],
            flops=6 * rows * part * wide * wide * pairs,
        )
        theirs = flip(theirs, "col", cols, 1)
        parts = [mine[e] + theirs[e] for e in range(pairs)]
        panel_core = sum(flip(parts[e], "col", cols, 2 * e) if e else parts[e] for e in range(pairs))
        panel_core = panel_core.reshape(tile_rows, rank_cap, rank_cap) / tile_order

        kept_cols = (columns[None, :] < trail_rank).astype(jnp.float32)[:, None, :]

        def to_tiles(block):
            return block.reshape(tile_rows, tile_order, rank_cap) * kept_cols

        tile_left = to_tiles(left)
        tile_right = to_tiles(right)
        tile_probe = to_tiles(probes)
        right_probe = dot("tnk,tnl->tkl", tile_right, tile_probe)
        tile_part = dot("tnk,tkl->tnl", tile_left, right_probe)
        panel_probe = dot("nk,tnl->tkl", col_left, tile_probe)
        core_probe = dot("tkl,tlm->tkm", panel_core, panel_probe)
        sampled = (tile_part - dot("tnk,tkl->tnl", row_left, core_probe)) / tile_order
        identity = (columns[:, None] == columns[None, :]).astype(jnp.float32)
        gram_matrix = dot("tnk,tnl->tkl", sampled, sampled)
        gram_matrix = gram_matrix + (1.0 - kept_cols) * identity
        inverse_gram = factor(gram_matrix)
        new_basis = dot("tnk,tlk->tnl", sampled, inverse_gram) * root_width
        left_proj = dot("tnk,tnl->tkl", tile_left, new_basis)
        panel_proj = dot("tnk,tnl->tkl", row_left, new_basis)
        core_proj = dot("tlk,tlm->tkm", panel_core, panel_proj)
        new_factor = (
            dot("tnk,tkl->tnl", tile_right, left_proj) - dot("nk,tkl->tnl", col_left, core_proj)
        ) / tile_order
        return (
            new_basis.reshape(tile_rows * tile_order, rank_cap),
            new_factor.reshape(tile_rows * tile_order, rank_cap),
        )

    return shards


def solution(mesh):
    return jax.shard_map(
        make_shards(mesh.shape["row"], mesh.shape["col"]),
        mesh=mesh,
        in_specs=(
            P(("row", "col"), None),
            P(("row", "col"), None),
            P(("row", "col"), None),
            P("row"),
            P("row", "col"),
            P("row", "col"),
            P("row", "col"),
            P("row", "col"),
        ),
        out_specs=(P("row", "col"), P("row", "col")),
        check_vma=False,
    )
```

```python
import math

import jax
import jax.numpy as jnp
from jax import lax
from jax.experimental import pallas as pl
from jax.experimental.pallas import tpu as pltpu
from jax.sharding import PartitionSpec as P

highest = lax.Precision.HIGHEST
SUB = 8


def split_three(x):
    a = x.astype(jnp.bfloat16)
    r = x - a.astype(jnp.float32)
    b = r.astype(jnp.bfloat16)
    c = (r - b.astype(jnp.float32)).astype(jnp.bfloat16)
    return a, b, c


def hot_dot(x, y, dims):
    return lax.dot_general(x, y, (dims, ((), ())), precision=lax.Precision.HIGHEST, preferred_element_type=jnp.float32)


def factor_blocks(block, scratch):
    count = len(block)
    n = block[0].shape[0]
    wide = 2 * n
    groups = n // SUB
    lane = lax.broadcasted_iota(jnp.int32, (SUB, wide), 1)
    sub = lax.broadcasted_iota(jnp.int32, (SUB, wide), 0)
    state = []
    for t in range(count):
        eye = [jnp.where(lane - n == sub + SUB * g, 1.0, 0.0) for g in range(groups)]
        full = jnp.concatenate([block[t], jnp.zeros((n, n), jnp.float32)], axis=1)
        state.append([full[SUB * g : SUB * (g + 1)] + eye[g] for g in range(groups)])
    out = [[None] * groups for _ in range(count)]
    for k in range(groups):
        for t in range(count):
            rows = state[t]
            spread = [
                [jnp.broadcast_to(rows[g][:, SUB * k + j : SUB * k + j + 1], (SUB, wide)) for j in range(SUB)]
                for g in range(k, groups)
            ]
            for j in range(SUB):
                scratch[t, j] = spread[0][j]
            scratch[t, SUB] = rows[k]
            a = [
                [jnp.broadcast_to(scratch[t, j, i : i + 1, :], (SUB, wide)) for j in range(i + 1)]
                for i in range(SUB)
            ]
            row = [jnp.broadcast_to(scratch[t, SUB, i : i + 1, :], (SUB, wide)) for i in range(SUB)]
            inv = [None] * SUB
            low = [[None] * SUB for _ in range(SUB)]
            for j in range(SUB):
                inv[j] = 1.0 / a[j][j]
                for i in range(j + 1, SUB):
                    low[i][j] = a[i][j] * inv[j]
                for i in range(j + 1, SUB):
                    for h in range(i, SUB):
                        a[h][i] = a[h][i] - low[h][j] * a[i][j]
                    row[i] = row[i] - low[i][j] * row[j]
            done = row[0] * lax.rsqrt(a[0][0])
            for i in range(1, SUB):
                done = jnp.where(sub == i, row[i] * lax.rsqrt(a[i][i]), done)
            out[t][k] = done
            for g in range(k + 1, groups):
                cols = spread[g - k]
                scaled = []
                value = rows[g]
                for j in range(SUB):
                    x = cols[j]
                    for h in range(j):
                        x = x - scaled[h] * a[j][h]
                    scaled.append(x * inv[j])
                    value = value - scaled[j] * row[j]
                rows[g] = value
    return [jnp.concatenate(o, axis=0)[:, n:] for o in out]


def inverse_factor(gram_of, put, order, step, scratch, count):
    work = [gram_of(t) for t in range(count)]
    eye = (
        lax.broadcasted_iota(jnp.int32, (order, order), 0) == lax.broadcasted_iota(jnp.int32, (order, order), 1)
    )
    scale = []
    for t in range(count):
        diag = jnp.where(eye, work[t], 0.0)
        down = lax.rsqrt(jnp.sum(diag, axis=1, keepdims=True))
        across = lax.rsqrt(jnp.sum(diag, axis=0, keepdims=True))
        scale.append(across)
        work[t] = jnp.concatenate([work[t] * down * across, jnp.where(eye, 1.0, 0.0)], axis=1)
    for k in range(order // step):
        lo = k * step
        inner = factor_blocks([w[:step, lo : lo + step] for w in work], scratch)
        for t in range(count):
            solved = hot_dot(inner[t], work[t][:step], ((1,), (0,)))
            put(t, lo, solved[:, order:] * scale[t])
            if lo + step < order:
                tail = solved[:, lo + step : order]
                work[t] = work[t][step:] - hot_dot(tail, solved, ((0,), (0,)))


def factor_kernel(gram_ref, out_ref, scratch):
    count, order, _ = gram_ref.shape

    def put(t, lo, value):
        out_ref[t, lo : lo + value.shape[0], :] = value

    inverse_factor(lambda t: gram_ref[t], put, order, 64, scratch, count)


def factor(gram, **kw):
    return pl.pallas_call(
        factor_kernel,
        out_shape=jax.ShapeDtypeStruct(gram.shape, jnp.float32),
        in_specs=[pl.BlockSpec(memory_space=pltpu.VMEM)],
        out_specs=pl.BlockSpec(memory_space=pltpu.VMEM),
        scratch_shapes=[pltpu.VMEM((gram.shape[0], SUB + 1, SUB, 128), jnp.float32)],
        compiler_params=pltpu.CompilerParams(vmem_limit_bytes=32 * 1024 * 1024),
        **kw,
    )(gram)


def flip(value, axis, size, mask):
    return lax.ppermute(value, axis, [(i, i ^ mask) for i in range(size)])


def after(value, *earlier):
    return lax.optimization_barrier((value, *earlier))[0]


def dot(spec, a, b):
    return jnp.einsum(spec, a, b, precision=highest, preferred_element_type=jnp.float32)


def shaped(shape, dtype=jnp.float32):
    return jax.ShapeDtypeStruct(shape, dtype)


def call(kernel, out, args, kinds, scratch=(), limit=60, flops=0):
    spaces = {"v": pltpu.VMEM, "s": pltpu.SMEM, "a": pl.ANY}
    moved = sum(a.size * a.dtype.itemsize for a in [*out, *args])
    return pl.pallas_call(
        kernel,
        out_shape=out,
        in_specs=[pl.BlockSpec(memory_space=spaces[k]) for k in kinds[: len(args)]],
        out_specs=[pl.BlockSpec(memory_space=spaces[k]) for k in kinds[len(args) :]],
        scratch_shapes=list(scratch),
        compiler_params=pltpu.CompilerParams(vmem_limit_bytes=limit * 1024 * 1024),
        cost_estimate=pl.CostEstimate(flops=flops, bytes_accessed=moved, transcendentals=0),
    )(*args)


def power_of_two(exponent):
    low = exponent + 128
    value = jnp.full(exponent.shape, 2.0**-64, jnp.float32)
    for bit in range(7):
        value = value * jnp.where((low >> bit) & 1 == 1, 2.0 ** (2**bit), 1.0)
    return value * jnp.where(low >= 128, 1.0, 2.0**-64) * jnp.where(low >= 128, 2.0**64, 1.0)


def packed_rows(rows):
    return rows // 4 * 3 + 8


def pack_into(value, out_ref):
    rows, width = value.shape
    piece = rows // 4
    top = jnp.max(jnp.abs(value), axis=0, keepdims=True)
    level = jnp.log(jnp.maximum(top, 2.0**-90)) * 1.4426950408889634
    exponent = jnp.floor(level).astype(jnp.int32) + 1
    factor_up = power_of_two(23 - exponent)
    limit = 2.0**23 - 1
    codes = [
        jnp.clip(jnp.round(value[piece * n : piece * (n + 1)] * factor_up), -limit, limit).astype(jnp.int32)
        for n in range(4)
    ]
    for n in range(3):
        out_ref[piece * n : piece * (n + 1), :] = (codes[n] << 8) | ((codes[3] >> (8 * n)) & 255)
    out_ref[3 * piece :, :] = jnp.broadcast_to(exponent, (8, width))


def unpack(words):
    rows, width = words.shape
    piece = (rows - 8) // 3
    part = [words[piece * n : piece * (n + 1)] for n in range(3)]
    down = power_of_two(words[3 * piece : 3 * piece + 1] - 23)
    last = ((part[2] << 24) | ((part[1] & 255) << 16) | ((part[0] & 255) << 8)) >> 8
    codes = [p >> 8 for p in part] + [last]
    return [c.astype(jnp.float32) * down for c in codes]


def load_all(pairs_of, sem):
    copies = [pltpu.make_async_copy(src, dst, sem.at[n]) for n, (src, dst) in enumerate(pairs_of)]
    for c in copies:
        c.start()
    for c in copies:
        c.wait()


def pack_kernel(value_ref, out_ref):
    pack_into(value_ref[...], out_ref)


def solve_kernel(rows, pairs, where_ref, rank_ref, *refs):
    inverse, held, other = refs[:rows], refs[rows : rows + pairs], refs[rows + pairs : rows + 2 * pairs]
    out_ref, packed_ref, whole, right, sem = refs[rows + 2 * pairs :]
    floor, me = where_ref[0], where_ref[1]
    part = inverse[0].shape[0]
    chunk, cap = held[0].shape
    quarters = pairs
    half, quarter = me // quarters, me % quarters
    moves = [
        (inverse[d], whole.at[pl.ds(pl.multiple_of((floor ^ d) * part, part), part), :]) for d in range(rows)
    ]
    for at in range(2 * pairs):
        moves.append((held[at // 2] if at % 2 == 0 else other[at // 2], right.at[at]))
    load_all(moves, sem)
    column = lax.broadcasted_iota(jnp.int32, (1, cap), 1)
    for h in range(2):
        total = None
        for d in range(quarters):
            lhs = whole[:, pl.ds(pl.multiple_of((quarter ^ d) * chunk, chunk), chunk)]
            for piece in split_three(right[h * quarters + d]):
                term = jnp.dot(lhs, piece, preferred_element_type=jnp.float32)
                total = term if total is None else total + term
        tile = half ^ h
        kept = column < rank_ref[tile]
        out_ref[:, pl.ds(pl.multiple_of(tile * cap, cap), cap)] = jnp.where(kept, total, 0.0)
    pack_into(out_ref[...], packed_ref)


def core_kernel(rows, pairs, where_ref, own_ref, *refs):
    arrived, (mine_ref, theirs_ref, solved, sem) = refs[: rows - 1], refs[rows - 1 :]
    floor, me = where_ref[0], where_ref[1]
    pair, side = me // 2, me % 2
    cap = mine_ref.shape[2]
    own = own_ref[...]
    load_all([(arrived[d], solved.at[d]) for d in range(rows - 1)], sem)

    def halves(x):
        high = x.astype(jnp.bfloat16)
        return high, (x - high.astype(jnp.float32)).astype(jnp.bfloat16)

    own_high, own_low = halves(own)

    own_high, own_low = own_high.T, own_low.T

    def across(x, y):
        return jnp.dot(x, y, preferred_element_type=jnp.float32)

    for e in range(pairs):
        wanted = floor ^ pair ^ e
        there = jnp.concatenate(unpack(solved[jnp.maximum(wanted, 1) - 1]), axis=0)
        high, low = halves(jnp.where(wanted == 0, own, there))
        part = across(own_high, high) + (across(own_high, low) + across(own_low, high))
        left, right = part[:, :cap], part[:, cap:]
        mine_ref[e] = jnp.where(side == 0, left, right)
        theirs_ref[e] = jnp.where(side == 0, right, left)


def choose_kernel(rows, pairs, where_ref, *refs):
    ins, outs = refs[:rows], refs[rows:]
    mark = where_ref[0] ^ (where_ref[1] // 2)
    for e in range(pairs):
        outs[e][0] = ins[0][...]
        for d in range(rows):

            @pl.when(mark == d ^ e)
            def _(d=d, e=e):
                outs[e][1] = ins[d][...]


def spread_kernel(pairs, where_ref, *refs):
    held, other, (row_ref, col_ref, words, sem) = refs[:pairs], refs[pairs : 2 * pairs], refs[2 * pairs :]
    me = where_ref[1]
    pair, side = me // 2, me % 2
    half = pairs // 2
    load_all([(ref, words.at[n]) for n, ref in enumerate([*held, *other])], sem)

    def put(ref, values, slot):
        piece = values[0].shape[0]
        for i in range(4):
            ref[pl.ds(pl.multiple_of(slot * (4 * piece) + piece * i, piece), piece), :] = values[i]

    for n in range(2 * pairs):
        put(row_ref, unpack(words[n, 0]), me ^ (2 * (n % pairs) + n // pairs))
    upper = (pair // half) ^ side
    for n in range(pairs):
        e = n % half + half * upper
        from_other = n // half
        put(col_ref, unpack(words[from_other * pairs + e, 1]), 2 * ((pair ^ e) % half) + (side ^ from_other))


def make_shards(rows, cols):
    pairs = cols // 2

    def shards(factor_inverse, panel_left, panel_right, panel_rank, left, right, probes, trail_rank):
        tile_rows, tile_cols = trail_rank.shape
        tile_order = factor_inverse.shape[1]
        rank_cap = left.shape[1] // tile_cols
        chunk = panel_left.shape[0]
        part = factor_inverse.shape[0]
        root_width = math.sqrt(tile_order)
        me = lax.axis_index("col").astype(jnp.int32)
        floor = lax.axis_index("row").astype(jnp.int32)
        spot = jnp.stack([floor, me])
        columns = jnp.arange(rank_cap, dtype=jnp.int32)
        my_pair, my_side = me // 2, me % 2
        wide = tile_rows * rank_cap

        words = call(pack_kernel, [shaped((packed_rows(chunk), rank_cap), jnp.int32)], [panel_left], "vv")[0]
        inverse = [factor_inverse] + [flip(factor_inverse, "row", rows, d) for d in range(1, rows)]
        held = [panel_right] + [flip(panel_right, "col", cols, 2 * e) for e in range(1, pairs)]
        held, inverse, words = lax.optimization_barrier((held, inverse, words))
        other = [flip(h, "col", cols, 1) for h in held]
        from_floors = [words] + [flip(words, "row", rows, d) for d in range(1, rows)]

        solved, solved_words = call(
            lambda *refs: solve_kernel(rows, pairs, *refs),
            [shaped((rows * part, wide)), shaped((packed_rows(rows * part), wide), jnp.int32)],
            [spot, panel_rank, *inverse, *held, *other],
            "ss" + "a" * (rows + 2 * pairs) + "vv",
            [
                pltpu.VMEM((rows * part, tile_order), jnp.bfloat16),
                pltpu.VMEM((cols, chunk, rank_cap), jnp.float32),
                pltpu.SemaphoreType.DMA((rows + cols,)),
            ],
            flops=6 * rows * part * tile_order * wide,
        )
        arrived = [flip(solved_words, "row", rows, d) for d in range(1, rows)]

        *from_floors, _ = lax.optimization_barrier((*from_floors, solved_words))
        mixed = call(
            lambda *refs: choose_kernel(rows, pairs, *refs),
            [shaped((2, *words.shape), jnp.int32)] * pairs,
            [spot, *from_floors],
            "s" + "v" * (rows + pairs),
        )
        mixed = [flip(mixed[e], "col", cols, 2 * e) if e else mixed[e] for e in range(pairs)]

        kept_cols = (columns[None, :] < trail_rank).astype(jnp.float32)[:, None, :]

        def to_tiles(block):
            return block.reshape(tile_rows, tile_order, rank_cap) * kept_cols

        tile_left = to_tiles(left)
        tile_right = to_tiles(right)
        tile_probe = to_tiles(probes)
        right_probe = dot("tnk,tnl->tkl", tile_right, tile_probe)
        tile_part = dot("tnk,tkl->tnl", tile_left, right_probe)
        mixed, arrived, tile_part = lax.optimization_barrier((mixed, arrived, tile_part))
        swapped = [flip(m, "col", cols, 1) for m in mixed]

        mine, theirs = call(
            lambda *refs: core_kernel(rows, pairs, *refs),
            [shaped((pairs, wide, rank_cap))] * 2,
            [spot, solved, *arrived],
            "sv" + "a" * (rows - 1) + "vv",
            [
                pltpu.VMEM((rows - 1, *solved_words.shape), jnp.int32),
                pltpu.SemaphoreType.DMA((rows - 1,)),
            ],
            flops=6 * rows * part * wide * wide * pairs,
        )
        theirs = flip(theirs, "col", cols, 1)
        parts = [mine[e] + theirs[e] for e in range(pairs)]
        swapped = lax.optimization_barrier((swapped, parts))[0]
        parts = [flip(parts[e], "col", cols, 2 * e) if e else parts[e] for e in range(pairs)]
        row_left, col_left = call(
            lambda *refs: spread_kernel(pairs, *refs),
            [shaped((cols * chunk, rank_cap)), shaped((pairs * chunk, rank_cap))],
            [spot, *mixed, *swapped],
            "s" + "a" * (2 * pairs) + "vv",
            [pltpu.VMEM((2 * pairs, 2, *words.shape), jnp.int32), pltpu.SemaphoreType.DMA((2 * pairs,))],
        )
        row_left = row_left.reshape(tile_rows, tile_order, rank_cap)

        panel_probe = dot("nk,tnl->tkl", col_left, tile_probe)
        parts, panel_probe, row_left = lax.optimization_barrier((parts, panel_probe, row_left))
        panel_core = sum(parts).reshape(tile_rows, rank_cap, rank_cap) / tile_order
        core_probe = dot("tkl,tlm->tkm", panel_core, panel_probe)
        sampled = (tile_part - dot("tnk,tkl->tnl", row_left, core_probe)) / tile_order
        identity = (columns[:, None] == columns[None, :]).astype(jnp.float32)
        gram_matrix = dot("tnk,tnl->tkl", sampled, sampled)
        gram_matrix = gram_matrix + (1.0 - kept_cols) * identity
        inverse_gram = factor(gram_matrix)
        new_basis = dot("tnk,tlk->tnl", sampled, inverse_gram) * root_width
        left_proj = dot("tnk,tnl->tkl", tile_left, new_basis)
        panel_proj = dot("tnk,tnl->tkl", row_left, new_basis)
        core_proj = dot("tlk,tlm->tkm", panel_core, panel_proj)
        new_factor = (
            dot("tnk,tkl->tnl", tile_right, left_proj) - dot("nk,tkl->tnl", col_left, core_proj)
        ) / tile_order
        return (
            new_basis.reshape(tile_rows * tile_order, rank_cap),
            new_factor.reshape(tile_rows * tile_order, rank_cap),
        )

    return shards


def solution(mesh):
    return jax.shard_map(
        make_shards(mesh.shape["row"], mesh.shape["col"]),
        mesh=mesh,
        in_specs=(
            P(("row", "col"), None),
            P(("row", "col"), None),
            P(("row", "col"), None),
            P("row"),
            P("row", "col"),
            P("row", "col"),
            P("row", "col"),
            P("row", "col"),
        ),
        out_specs=(P("row", "col"), P("row", "col")),
        check_vma=False,
    )
```

```python
import math

import jax
import jax.numpy as jnp
from jax import lax
from jax.experimental import pallas as pl
from jax.experimental.pallas import tpu as pltpu
from jax.sharding import PartitionSpec as P

highest = lax.Precision.HIGHEST
SUB = 8


def split_three(x):
    a = x.astype(jnp.bfloat16)
    r = x - a.astype(jnp.float32)
    b = r.astype(jnp.bfloat16)
    c = (r - b.astype(jnp.float32)).astype(jnp.bfloat16)
    return a, b, c


def hot_dot(x, y, dims):
    return lax.dot_general(x, y, (dims, ((), ())), precision=lax.Precision.HIGHEST, preferred_element_type=jnp.float32)


def factor_blocks(block, scratch):
    count = len(block)
    n = block[0].shape[0]
    wide = 2 * n
    groups = n // SUB
    lane = lax.broadcasted_iota(jnp.int32, (SUB, wide), 1)
    sub = lax.broadcasted_iota(jnp.int32, (SUB, wide), 0)
    state = []
    for t in range(count):
        eye = [jnp.where(lane - n == sub + SUB * g, 1.0, 0.0) for g in range(groups)]
        full = jnp.concatenate([block[t], jnp.zeros((n, n), jnp.float32)], axis=1)
        state.append([full[SUB * g : SUB * (g + 1)] + eye[g] for g in range(groups)])
    out = [[None] * groups for _ in range(count)]
    for k in range(groups):
        for t in range(count):
            rows = state[t]
            spread = [
                [jnp.broadcast_to(rows[g][:, SUB * k + j : SUB * k + j + 1], (SUB, wide)) for j in range(SUB)]
                for g in range(k, groups)
            ]
            for j in range(SUB):
                scratch[t, j] = spread[0][j]
            scratch[t, SUB] = rows[k]
            a = [
                [jnp.broadcast_to(scratch[t, j, i : i + 1, :], (SUB, wide)) for j in range(i + 1)]
                for i in range(SUB)
            ]
            row = [jnp.broadcast_to(scratch[t, SUB, i : i + 1, :], (SUB, wide)) for i in range(SUB)]
            inv = [None] * SUB
            low = [[None] * SUB for _ in range(SUB)]
            for j in range(SUB):
                inv[j] = 1.0 / a[j][j]
                for i in range(j + 1, SUB):
                    low[i][j] = a[i][j] * inv[j]
                for i in range(j + 1, SUB):
                    for h in range(i, SUB):
                        a[h][i] = a[h][i] - low[h][j] * a[i][j]
                    row[i] = row[i] - low[i][j] * row[j]
            done = row[0] * lax.rsqrt(a[0][0])
            for i in range(1, SUB):
                done = jnp.where(sub == i, row[i] * lax.rsqrt(a[i][i]), done)
            out[t][k] = done
            for g in range(k + 1, groups):
                cols = spread[g - k]
                scaled = []
                value = rows[g]
                for j in range(SUB):
                    x = cols[j]
                    for h in range(j):
                        x = x - scaled[h] * a[j][h]
                    scaled.append(x * inv[j])
                    value = value - scaled[j] * row[j]
                rows[g] = value
    return [jnp.concatenate(o, axis=0)[:, n:] for o in out]


def inverse_factor(gram_of, put, order, step, scratch, count):
    work = [gram_of(t) for t in range(count)]
    eye = (
        lax.broadcasted_iota(jnp.int32, (order, order), 0) == lax.broadcasted_iota(jnp.int32, (order, order), 1)
    )
    scale = []
    for t in range(count):
        diag = jnp.where(eye, work[t], 0.0)
        down = lax.rsqrt(jnp.sum(diag, axis=1, keepdims=True))
        across = lax.rsqrt(jnp.sum(diag, axis=0, keepdims=True))
        scale.append(across)
        work[t] = jnp.concatenate([work[t] * down * across, jnp.where(eye, 1.0, 0.0)], axis=1)
    for k in range(order // step):
        lo = k * step
        inner = factor_blocks([w[:step, lo : lo + step] for w in work], scratch)
        for t in range(count):
            solved = hot_dot(inner[t], work[t][:step], ((1,), (0,)))
            put(t, lo, solved[:, order:] * scale[t])
            if lo + step < order:
                tail = solved[:, lo + step : order]
                work[t] = work[t][step:] - hot_dot(tail, solved, ((0,), (0,)))


def flip(value, axis, size, mask):
    return lax.ppermute(value, axis, [(i, i ^ mask) for i in range(size)])


def floor_gather(block, size):
    got = {0: block}
    for d in sorted(range(1, size), key=lambda d: (bin(d).count("1"), d)):
        got[d] = flip(got[d & (d - 1)], "row", size, d & -d)
    return [got[d] for d in range(size)]


def after(value, *earlier):
    return lax.optimization_barrier((value, *earlier))[0]


def dot(spec, a, b):
    return jnp.einsum(spec, a, b, precision=highest, preferred_element_type=jnp.float32)


def shaped(shape, dtype=jnp.float32):
    return jax.ShapeDtypeStruct(shape, dtype)


def call(kernel, out, args, kinds, scratch=(), limit=60, flops=0):
    spaces = {"v": pltpu.VMEM, "s": pltpu.SMEM, "a": pl.ANY}
    moved = sum(a.size * a.dtype.itemsize for a in [*out, *args])
    return pl.pallas_call(
        kernel,
        out_shape=out,
        in_specs=[pl.BlockSpec(memory_space=spaces[k]) for k in kinds[: len(args)]],
        out_specs=[pl.BlockSpec(memory_space=spaces[k]) for k in kinds[len(args) :]],
        scratch_shapes=list(scratch),
        compiler_params=pltpu.CompilerParams(vmem_limit_bytes=limit * 1024 * 1024),
        cost_estimate=pl.CostEstimate(flops=flops, bytes_accessed=moved, transcendentals=0),
    )(*args)


def power_of_two(exponent):
    low = exponent + 128
    value = jnp.full(exponent.shape, 2.0**-64, jnp.float32)
    for bit in range(7):
        value = value * jnp.where((low >> bit) & 1 == 1, 2.0 ** (2**bit), 1.0)
    return value * jnp.where(low >= 128, 1.0, 2.0**-64) * jnp.where(low >= 128, 2.0**64, 1.0)


def packed_rows(rows):
    return rows // 4 * 3 + 8


def pack_into(value, out_ref):
    rows, width = value.shape
    piece = rows // 4
    top = jnp.max(jnp.abs(value), axis=0, keepdims=True)
    level = jnp.log(jnp.maximum(top, 2.0**-90)) * 1.4426950408889634
    exponent = jnp.floor(level).astype(jnp.int32) + 1
    factor_up = power_of_two(23 - exponent)
    limit = 2.0**23 - 1
    codes = [
        jnp.clip(jnp.round(value[piece * n : piece * (n + 1)] * factor_up), -limit, limit).astype(jnp.int32)
        for n in range(4)
    ]
    for n in range(3):
        out_ref[piece * n : piece * (n + 1), :] = (codes[n] << 8) | ((codes[3] >> (8 * n)) & 255)
    out_ref[3 * piece :, :] = jnp.broadcast_to(exponent, (8, width))


def byte_planes(words):
    piece = (words.shape[0] - 8) // 3
    part = [words[piece * n : piece * (n + 1)] for n in range(3)]
    planes = [
        [p >> 24 for p in part] + [(part[2] << 24) >> 24],
        [(p >> 16) & 255 for p in part] + [part[1] & 255],
        [(p >> 8) & 255 for p in part] + [part[0] & 255],
    ]
    whole = [jnp.concatenate([x.astype(jnp.float32) for x in p], axis=0).astype(jnp.bfloat16) for p in planes]
    return whole, power_of_two(words[3 * piece : 3 * piece + 1] - 23)


def unpack(words):
    rows, width = words.shape
    piece = (rows - 8) // 3
    part = [words[piece * n : piece * (n + 1)] for n in range(3)]
    down = power_of_two(words[3 * piece : 3 * piece + 1] - 23)
    last = ((part[2] << 24) | ((part[1] & 255) << 16) | ((part[0] & 255) << 8)) >> 8
    codes = [p >> 8 for p in part] + [last]
    return [c.astype(jnp.float32) * down for c in codes]


def load_all(pairs_of, sem):
    copies = [pltpu.make_async_copy(src, dst, sem.at[n]) for n, (src, dst) in enumerate(pairs_of)]
    for c in copies:
        c.start()
    for c in copies:
        c.wait()


def pack_kernel(right_ref, left_ref, both_ref, left_words_ref):
    pack_into(right_ref[...], both_ref.at[0])
    pack_into(left_ref[...], left_words_ref)
    both_ref[1] = left_words_ref[...]


def solve_kernel(rows, pairs, where_ref, rank_ref, *refs):
    inverse, held, other = refs[:rows], refs[rows : rows + pairs], refs[rows + pairs : rows + 2 * pairs]
    out_ref, packed_ref, whole, right, sem = refs[rows + 2 * pairs :]
    floor, me = where_ref[0], where_ref[1]
    part = inverse[0].shape[0]
    words, cap = held[0].shape[1:]
    chunk = (words - 8) // 3 * 4
    quarters = pairs
    half, quarter = me // quarters, me % quarters
    moves = [
        (inverse[d], whole.at[pl.ds(pl.multiple_of((floor ^ d) * part, part), part), :]) for d in range(rows)
    ]
    for at in range(2 * pairs):
        moves.append(((held if at % 2 == 0 else other)[at // 2].at[0], right.at[at]))
    load_all(moves, sem)
    column = lax.broadcasted_iota(jnp.int32, (1, cap), 1)
    for h in range(2):
        total = None
        for d in range(quarters):
            lhs = whole[:, pl.ds(pl.multiple_of((quarter ^ d) * chunk, chunk), chunk)]
            planes, scale = byte_planes(right[h * quarters + d])
            term = 0.0
            for plane in planes:
                term = term * 256.0 + jnp.dot(lhs, plane, preferred_element_type=jnp.float32)
            term = term * scale
            total = term if total is None else total + term
        tile = half ^ h
        kept = column < rank_ref[tile]
        out_ref[:, pl.ds(pl.multiple_of(tile * cap, cap), cap)] = jnp.where(kept, total, 0.0)
    pack_into(out_ref[...], packed_ref)


def core_kernel(rows, pairs, where_ref, own_ref, *refs):
    arrived, (mine_ref, theirs_ref, solved, sem) = refs[: rows - 1], refs[rows - 1 :]
    floor, me = where_ref[0], where_ref[1]
    pair, side = me // 2, me % 2
    cap = mine_ref.shape[2]
    own = own_ref[...]
    load_all([(arrived[d], solved.at[d]) for d in range(rows - 1)], sem)

    def halves(x):
        high = x.astype(jnp.bfloat16)
        return high, (x - high.astype(jnp.float32)).astype(jnp.bfloat16)

    own_high, own_low = halves(own)

    own_high, own_low = own_high.T, own_low.T

    def across(x, y):
        return jnp.dot(x, y, preferred_element_type=jnp.float32)

    for e in range(pairs):
        wanted = floor ^ pair ^ e
        there = jnp.concatenate(unpack(solved[jnp.maximum(wanted, 1) - 1]), axis=0)
        high, low = halves(jnp.where(wanted == 0, own, there))
        part = across(own_high, high) + (across(own_high, low) + across(own_low, high))
        left, right = part[:, :cap], part[:, cap:]
        mine_ref[e] = jnp.where(side == 0, left, right)
        theirs_ref[e] = jnp.where(side == 0, right, left)


def choose_kernel(rows, pairs, where_ref, *refs):
    ins, outs = refs[:rows], refs[rows:]
    mark = where_ref[0] ^ (where_ref[1] // 2)
    for e in range(pairs):
        for d in range(rows):

            @pl.when(mark == d ^ e)
            def _(d=d, e=e):
                outs[e][...] = ins[d][...]


def fold_kernel(pairs, mine_ref, theirs_ref, own_ref, *outs):
    own_ref[...] = mine_ref[0] + theirs_ref[0]
    for e in range(1, pairs):
        pack_into(mine_ref[e] + theirs_ref[e], outs[e - 1])


def spread_kernel(pairs, where_ref, *refs):
    row_in, col_in = refs[: 2 * pairs], refs[2 * pairs : 4 * pairs]
    row_ref, col_ref, col_pieces, words, sem = refs[4 * pairs :]
    me = where_ref[1]
    pair, side = me // 2, me % 2
    half = pairs // 2
    moves = [(ref.at[1], words.at[n, 0]) for n, ref in enumerate(row_in)]
    load_all(moves + [(ref, words.at[n, 1]) for n, ref in enumerate(col_in)], sem)

    def put(values, slot, count, pieces, whole=None):
        piece, cap = values[0].shape
        for i in range(4):
            at = pl.ds(pl.multiple_of(slot * (4 * piece) + piece * i, piece), piece)
            if whole is not None:
                whole[at, :] = values[i]
            for n, value in enumerate(split_three(values[i])[:count]):
                pieces[at, n * cap : (n + 1) * cap] = value

    for n in range(2 * pairs):
        put(unpack(words[n, 0]), me ^ (2 * (n % pairs) + n // pairs), 3, row_ref)
    upper = (pair // half) ^ side
    for n in range(pairs):
        e = n % half + half * upper
        from_other = n // half
        slot = 2 * ((pair ^ e) % half) + (side ^ from_other)
        put(unpack(words[from_other * pairs + e, 1]), slot, 2, col_pieces, col_ref)


def stacked(pieces, picks):
    return jnp.concatenate([pieces[n] for n in picks], axis=0)


def wide_six(lhs, right):
    cap = right.shape[0]
    r = split_three(right)
    total = jnp.dot(lhs, stacked(r, (0, 0, 0)), preferred_element_type=jnp.float32)
    total += jnp.dot(lhs[:, : 2 * cap], stacked(r, (1, 1)), preferred_element_type=jnp.float32)
    return total + jnp.dot(lhs[:, :cap], r[2], preferred_element_type=jnp.float32)


def wide_three(lhs, right):
    cap = right.shape[0]
    r = split_three(right)
    total = jnp.dot(lhs, stacked(r, (0, 0)), preferred_element_type=jnp.float32)
    return total + jnp.dot(lhs[:, :cap], r[1], preferred_element_type=jnp.float32)


def over_rows(x, y):
    return lax.dot_general(x, y, (((0,), (0,)), ((), ())), preferred_element_type=jnp.float32)


def local_kernel(rank_ref, left_ref, right_ref, probe_ref, part_ref, left_pieces, right_pieces):
    tiles, order, cap = left_ref.shape
    step = order // 4
    row = lax.broadcasted_iota(jnp.int32, (cap, cap), 0)
    column = lax.broadcasted_iota(jnp.int32, (cap, cap), 1)
    for t in range(tiles):
        product = jnp.zeros((cap, cap), jnp.float32)
        for s in range(0, order, step):
            product += hot_dot(right_ref[t, s : s + step], probe_ref[t, s : s + step], ((0,), (0,)))
        rank = rank_ref[t, 0]
        product = jnp.where((row < rank) & (column < rank), product, 0.0) / order
        for s in range(0, order, step):
            at = slice(s, s + step)
            part_ref[t, at, :] = hot_dot(left_ref[t, at], product, ((1,), (0,)))
            for ref, out in ((left_ref, left_pieces), (right_ref, right_pieces)):
                for n, value in enumerate(split_three(ref[t, at])[:2]):
                    out[t, at, n * cap : (n + 1) * cap] = value


def final_kernel(parts, rank_ref, probe_ref, *refs):
    cores = refs[:parts]
    tall = refs[parts : parts + 5]
    basis_out, factor_out = refs[parts + 5 : parts + 7]
    part, panel, left, right, col, sampled, basis, outs, inverse, scratch, sem, sem_out = refs[parts + 7 :]
    tiles, order, cap = part.shape
    step = order // 4
    loads = []
    for t in range(tiles):
        for src, dst in ((tall[0], part), (tall[1], panel)):
            loads.append(pltpu.make_async_copy(src.at[t], dst.at[t], sem.at[len(loads)]))
    for src, dst in ((tall[2], left), (tall[3], right), (tall[4], col)):
        loads.append(pltpu.make_async_copy(src, dst, sem.at[len(loads)]))
    for c in loads:
        c.start()
    root = math.sqrt(order)
    row = lax.broadcasted_iota(jnp.int32, (cap, cap), 0)
    column = lax.broadcasted_iota(jnp.int32, (cap, cap), 1)

    total = cores[0][...]
    for c in cores[1:]:
        total = total + jnp.concatenate(unpack(c[...]), axis=0)

    def core(t):
        return total[t * cap : (t + 1) * cap] / order

    grams = []
    for t in range(tiles):
        weight = hot_dot(core(t), probe_ref[t], ((1,), (0,))) / order
        loads[2 * t].wait()
        loads[2 * t + 1].wait()
        same = jnp.zeros((cap, cap), jnp.float32)
        cross = jnp.zeros((cap, cap), jnp.float32)
        for s in range(0, order, step):
            at = slice(s, s + step)
            value = part[t, at] - wide_six(panel[t, at], weight)
            pieces = split_three(value)
            for n in range(3):
                sampled[t, at, n * cap : (n + 1) * cap] = pieces[n]
            product = over_rows(pieces[0], sampled[t, at])
            same += product[:, :cap] + over_rows(pieces[1], pieces[1])
            cross += product[:, cap : 2 * cap] + product[:, 2 * cap :]
        gram = same + (cross + cross.T)
        grams.append(gram + jnp.where((row == column) & (column >= rank_ref[t, 0]), 1.0, 0.0))

    def put(t, lo, value):
        inverse[t, lo : lo + value.shape[0], :] = value

    inverse_factor(lambda t: grams[t], put, cap, 64, scratch, tiles)
    for c in loads[2 * tiles :]:
        c.wait()
    sends = []
    for t in range(tiles):
        weight = inverse[t].T * root
        left_proj = jnp.zeros((cap, cap), jnp.float32)
        panel_proj = jnp.zeros((cap, cap), jnp.float32)
        for s in range(0, order, step):
            at = slice(s, s + step)
            value = wide_six(sampled[t, at], weight)
            outs[t, at, :] = value
            high, low, _ = split_three(value)
            one = over_rows(high, left[t, at])
            left_proj += one[:, :cap] + one[:, cap:] + over_rows(low, left[t, at, :cap])
            one = over_rows(high, panel[t, at, : 2 * cap])
            panel_proj += one[:, :cap] + one[:, cap:] + over_rows(low, panel[t, at, :cap])
        sends.append(pltpu.make_async_copy(outs.at[t], basis_out.at[t], sem_out.at[t]))
        sends[-1].start()
        left_proj = jnp.where(column < rank_ref[t, 0], left_proj, 0.0).T / order
        core_proj = hot_dot(core(t), panel_proj, ((0,), (1,))) / order
        for s in range(0, order, step):
            at = slice(s, s + step)
            basis[t, at, :] = wide_three(right[t, at], left_proj) - wide_three(col[at], core_proj)
        sends.append(pltpu.make_async_copy(basis.at[t], factor_out.at[t], sem_out.at[tiles + t]))
        sends[-1].start()
    for c in sends:
        c.wait()


def make_shards(rows, cols):
    pairs = cols // 2

    def shards(factor_inverse, panel_left, panel_right, panel_rank, left, right, probes, trail_rank):
        tile_rows, tile_cols = trail_rank.shape
        tile_order = factor_inverse.shape[1]
        rank_cap = left.shape[1] // tile_cols
        chunk = panel_left.shape[0]
        part = factor_inverse.shape[0]
        me = lax.axis_index("col").astype(jnp.int32)
        floor = lax.axis_index("row").astype(jnp.int32)
        spot = jnp.stack([floor, me])
        columns = jnp.arange(rank_cap, dtype=jnp.int32)
        my_pair, my_side = me // 2, me % 2
        wide = tile_rows * rank_cap

        words_shape = (packed_rows(chunk), rank_cap)
        both, words = call(
            pack_kernel,
            [shaped((2, *words_shape), jnp.int32), shaped(words_shape, jnp.int32)],
            [panel_right, panel_left],
            "vvvv",
        )
        inverse = floor_gather(factor_inverse, rows)
        words = after(words, *inverse[1:])
        held = [both] + [flip(both, "col", cols, 2 * e) for e in range(1, pairs)]
        from_floors = floor_gather(words, rows)
        first = [d for d in range(rows) if d & (d - 1) == 0]
        held, inverse, _ = lax.optimization_barrier((held, inverse, [from_floors[d] for d in first]))
        other = [flip(h, "col", cols, 1) for h in held]

        solved, solved_words = call(
            lambda *refs: solve_kernel(rows, pairs, *refs),
            [shaped((rows * part, wide)), shaped((packed_rows(rows * part), wide), jnp.int32)],
            [spot, panel_rank, *inverse, *held, *other],
            "ss" + "a" * (rows + 2 * pairs) + "vv",
            [
                pltpu.VMEM((rows * part, tile_order), jnp.bfloat16),
                pltpu.VMEM((cols, *words_shape), jnp.int32),
                pltpu.SemaphoreType.DMA((rows + cols,)),
            ],
            flops=6 * rows * part * tile_order * wide,
        )
        arrived = floor_gather(solved_words, rows)[1:]

        *from_floors, _ = lax.optimization_barrier((*from_floors, solved_words))
        mixed = call(
            lambda *refs: choose_kernel(rows, pairs, *refs),
            [shaped(words_shape, jnp.int32)] * pairs,
            [spot, *from_floors],
            "s" + "v" * (rows + pairs),
        )
        mixed = [flip(mixed[e], "col", cols, 2 * e) if e else mixed[e] for e in range(pairs)]

        tall = (tile_rows, tile_order, rank_cap)
        pieces = lambda n: shaped((tile_rows, tile_order, n * rank_cap), jnp.bfloat16)
        tile_part, left_pieces, right_pieces = call(
            local_kernel,
            [shaped(tall), pieces(2), pieces(2)],
            [trail_rank, left.reshape(tall), right.reshape(tall), probes.reshape(tall)],
            "svvvvvv",
            flops=24 * tile_rows * tile_order * rank_cap * rank_cap,
        )
        mixed, arrived, tile_part = lax.optimization_barrier((mixed, arrived, tile_part))
        swapped = [flip(m, "col", cols, 1) for m in mixed]

        mine, theirs = call(
            lambda *refs: core_kernel(rows, pairs, *refs),
            [shaped((pairs, wide, rank_cap))] * 2,
            [spot, solved, *arrived],
            "sv" + "a" * (rows - 1) + "vv",
            [
                pltpu.VMEM((rows - 1, *solved_words.shape), jnp.int32),
                pltpu.SemaphoreType.DMA((rows - 1,)),
            ],
            flops=6 * rows * part * wide * wide * pairs,
        )
        theirs = flip(theirs, "col", cols, 1)
        parts = call(
            lambda *refs: fold_kernel(pairs, *refs),
            [shaped((wide, rank_cap))] + [shaped((packed_rows(wide), rank_cap), jnp.int32)] * (pairs - 1),
            [mine, theirs],
            "vv" + "v" * pairs,
        )
        swapped = lax.optimization_barrier((swapped, parts))[0]
        parts = [flip(parts[e], "col", cols, 2 * e) if e else parts[e] for e in range(pairs)]
        panel_pieces, col_left, col_pieces = call(
            lambda *refs: spread_kernel(pairs, *refs),
            [
                shaped((cols * chunk, 3 * rank_cap), jnp.bfloat16),
                shaped((pairs * chunk, rank_cap)),
                shaped((pairs * chunk, 2 * rank_cap), jnp.bfloat16),
            ],
            [spot, *held, *other, *mixed, *swapped],
            "s" + "a" * (4 * pairs) + "vvv",
            [pltpu.VMEM((2 * pairs, 2, *words_shape), jnp.int32), pltpu.SemaphoreType.DMA((4 * pairs,))],
        )
        panel_probe = dot("nk,tnl->tkl", col_left, probes.reshape(tall))
        panel_probe = jnp.where(columns[None, None, :] < trail_rank[:, :, None], panel_probe, 0.0)
        parts, panel_probe, panel_pieces = lax.optimization_barrier((parts, panel_probe, panel_pieces))

        new_basis, new_factor = call(
            lambda *refs: final_kernel(pairs, *refs),
            [shaped(tall), shaped(tall)],
            [
                trail_rank,
                panel_probe,
                *parts,
                tile_part,
                panel_pieces.reshape(tile_rows, tile_order, 3 * rank_cap),
                left_pieces,
                right_pieces,
                col_pieces,
            ],
            "sv" + "v" * pairs + "aaaaa" + "aa",
            [
                pltpu.VMEM(tall, jnp.float32),
                pltpu.VMEM((tile_rows, tile_order, 3 * rank_cap), jnp.bfloat16),
                pltpu.VMEM((tile_rows, tile_order, 2 * rank_cap), jnp.bfloat16),
                pltpu.VMEM((tile_rows, tile_order, 2 * rank_cap), jnp.bfloat16),
                pltpu.VMEM((tile_order, 2 * rank_cap), jnp.bfloat16),
                pltpu.VMEM((tile_rows, tile_order, 3 * rank_cap), jnp.bfloat16),
                pltpu.VMEM(tall, jnp.float32),
                pltpu.VMEM(tall, jnp.float32),
                pltpu.VMEM((tile_rows, rank_cap, rank_cap), jnp.float32),
                pltpu.VMEM((tile_rows, SUB + 1, SUB, 128), jnp.float32),
                pltpu.SemaphoreType.DMA((2 * tile_rows + 3,)),
                pltpu.SemaphoreType.DMA((2 * tile_rows,)),
            ],
            flops=60 * tile_rows * tile_order * rank_cap * rank_cap,
        )
        return (
            new_basis.reshape(tile_rows * tile_order, rank_cap),
            new_factor.reshape(tile_rows * tile_order, rank_cap),
        )

    return shards


def solution(mesh):
    return jax.shard_map(
        make_shards(mesh.shape["row"], mesh.shape["col"]),
        mesh=mesh,
        in_specs=(
            P(("row", "col"), None),
            P(("row", "col"), None),
            P(("row", "col"), None),
            P("row"),
            P("row", "col"),
            P("row", "col"),
            P("row", "col"),
            P("row", "col"),
        ),
        out_specs=(P("row", "col"), P("row", "col")),
        check_vma=False,
    )
```

```python
import functools
import math

import jax
import jax.numpy as jnp
from jax import lax
from jax.experimental import pallas as pl
from jax.experimental.pallas import tpu as pltpu
from jax.sharding import PartitionSpec as P

highest = lax.Precision.HIGHEST
SUB = 8


def split_three(x):
    a = x.astype(jnp.bfloat16)
    r = x - a.astype(jnp.float32)
    b = r.astype(jnp.bfloat16)
    c = (r - b.astype(jnp.float32)).astype(jnp.bfloat16)
    return a, b, c


def hot_dot(x, y, dims):
    return lax.dot_general(x, y, (dims, ((), ())), precision=lax.Precision.HIGHEST, preferred_element_type=jnp.float32)


def factor_blocks(block, scratch):
    count = len(block)
    n = block[0].shape[0]
    wide = 2 * n
    groups = n // SUB
    lane = lax.broadcasted_iota(jnp.int32, (SUB, wide), 1)
    sub = lax.broadcasted_iota(jnp.int32, (SUB, wide), 0)
    state = []
    for t in range(count):
        eye = [jnp.where(lane - n == sub + SUB * g, 1.0, 0.0) for g in range(groups)]
        full = jnp.concatenate([block[t], jnp.zeros((n, n), jnp.float32)], axis=1)
        state.append([full[SUB * g : SUB * (g + 1)] + eye[g] for g in range(groups)])
    out = [[None] * groups for _ in range(count)]
    for k in range(groups):
        for t in range(count):
            rows = state[t]
            spread = [
                [jnp.broadcast_to(rows[g][:, SUB * k + j : SUB * k + j + 1], (SUB, wide)) for j in range(SUB)]
                for g in range(k, groups)
            ]
            for j in range(SUB):
                scratch[t, j] = spread[0][j]
            scratch[t, SUB] = rows[k]
            a = [
                [jnp.broadcast_to(scratch[t, j, i : i + 1, :], (SUB, wide)) for j in range(i + 1)]
                for i in range(SUB)
            ]
            row = [jnp.broadcast_to(scratch[t, SUB, i : i + 1, :], (SUB, wide)) for i in range(SUB)]
            inv = [None] * SUB
            low = [[None] * SUB for _ in range(SUB)]
            for j in range(SUB):
                inv[j] = 1.0 / a[j][j]
                for i in range(j + 1, SUB):
                    low[i][j] = a[i][j] * inv[j]
                for i in range(j + 1, SUB):
                    for h in range(i, SUB):
                        a[h][i] = a[h][i] - low[h][j] * a[i][j]
                    row[i] = row[i] - low[i][j] * row[j]
            done = row[0] * lax.rsqrt(a[0][0])
            for i in range(1, SUB):
                done = jnp.where(sub == i, row[i] * lax.rsqrt(a[i][i]), done)
            out[t][k] = done
            for g in range(k + 1, groups):
                cols = spread[g - k]
                scaled = []
                value = rows[g]
                for j in range(SUB):
                    x = cols[j]
                    for h in range(j):
                        x = x - scaled[h] * a[j][h]
                    scaled.append(x * inv[j])
                    value = value - scaled[j] * row[j]
                rows[g] = value
    return [jnp.concatenate(o, axis=0)[:, n:] for o in out]


def inverse_factor(gram_of, put, order, step, scratch, count):
    work = [gram_of(t) for t in range(count)]
    eye = (
        lax.broadcasted_iota(jnp.int32, (order, order), 0) == lax.broadcasted_iota(jnp.int32, (order, order), 1)
    )
    scale = []
    for t in range(count):
        diag = jnp.where(eye, work[t], 0.0)
        down = lax.rsqrt(jnp.sum(diag, axis=1, keepdims=True))
        across = lax.rsqrt(jnp.sum(diag, axis=0, keepdims=True))
        scale.append(across)
        work[t] = jnp.concatenate([work[t] * down * across, jnp.where(eye, 1.0, 0.0)], axis=1)
    for k in range(order // step):
        lo = k * step
        inner = factor_blocks([w[:step, lo : lo + step] for w in work], scratch)
        for t in range(count):
            solved = hot_dot(inner[t], work[t][:step], ((1,), (0,)))
            put(t, lo, solved[:, order:] * scale[t])
            if lo + step < order:
                tail = solved[:, lo + step : order]
                work[t] = work[t][step:] - hot_dot(tail, solved, ((0,), (0,)))


def flip(value, axis, size, mask):
    return lax.ppermute(value, axis, [(i, i ^ mask) for i in range(size)])


def floor_gather(block, size):
    got = {0: block}
    got.update({d: flip(block, "row", size, d) for d in range(1, size) if d & (d - 1) == 0})

    def rest(got):
        got = dict(got)
        for d in sorted(set(range(1, size)) - set(got), key=lambda d: (bin(d).count("1"), d)):
            got[d] = flip(got[d & (d - 1)], "row", size, d & -d)
        return [got[d] for d in range(size)]

    return got, rest


def after(value, *earlier):
    return lax.optimization_barrier((value, *earlier))[0]


def dot(spec, a, b):
    return jnp.einsum(spec, a, b, precision=highest, preferred_element_type=jnp.float32)


def shaped(shape, dtype=jnp.float32):
    return jax.ShapeDtypeStruct(shape, dtype)


def call(kernel, out, args, kinds, scratch=(), limit=60, flops=0):
    spaces = {"v": pltpu.VMEM, "s": pltpu.SMEM, "a": pl.ANY}
    moved = sum(a.size * a.dtype.itemsize for a in [*out, *args])
    return pl.pallas_call(
        kernel,
        out_shape=out,
        in_specs=[pl.BlockSpec(memory_space=spaces[k]) for k in kinds[: len(args)]],
        out_specs=[pl.BlockSpec(memory_space=spaces[k]) for k in kinds[len(args) :]],
        scratch_shapes=list(scratch),
        compiler_params=pltpu.CompilerParams(vmem_limit_bytes=limit * 1024 * 1024),
        cost_estimate=pl.CostEstimate(flops=flops, bytes_accessed=moved, transcendentals=0),
    )(*args)


def power_of_two(exponent):
    low = exponent + 128
    value = jnp.full(exponent.shape, 2.0**-64, jnp.float32)
    for bit in range(7):
        value = value * jnp.where((low >> bit) & 1 == 1, 2.0 ** (2**bit), 1.0)
    return value * jnp.where(low >= 128, 1.0, 2.0**-64) * jnp.where(low >= 128, 2.0**64, 1.0)


def packed_rows(rows):
    return rows // 4 * 3 + 8


def pack_into(value, out_ref):
    rows, width = value.shape
    piece = rows // 4
    top = jnp.max(jnp.abs(value), axis=0, keepdims=True)
    level = jnp.log(jnp.maximum(top, 2.0**-90)) * 1.4426950408889634
    exponent = jnp.floor(level).astype(jnp.int32) + 1
    factor_up = power_of_two(23 - exponent)
    limit = 2.0**23 - 1
    codes = [
        jnp.clip(jnp.round(value[piece * n : piece * (n + 1)] * factor_up), -limit, limit).astype(jnp.int32)
        for n in range(4)
    ]
    for n in range(3):
        out_ref[piece * n : piece * (n + 1), :] = (codes[n] << 8) | ((codes[3] >> (8 * n)) & 255)
    out_ref[3 * piece :, :] = jnp.broadcast_to(exponent, (8, width))


def byte_planes(words):
    piece = (words.shape[0] - 8) // 3
    part = [words[piece * n : piece * (n + 1)] for n in range(3)]
    planes = [
        [p >> 24 for p in part] + [(part[2] << 24) >> 24],
        [(p >> 16) & 255 for p in part] + [part[1] & 255],
        [(p >> 8) & 255 for p in part] + [part[0] & 255],
    ]
    whole = [jnp.concatenate([x.astype(jnp.float32) for x in p], axis=0).astype(jnp.bfloat16) for p in planes]
    return whole, power_of_two(words[3 * piece : 3 * piece + 1] - 23)


def unpack(words):
    rows, width = words.shape
    piece = (rows - 8) // 3
    part = [words[piece * n : piece * (n + 1)] for n in range(3)]
    down = power_of_two(words[3 * piece : 3 * piece + 1] - 23)
    last = ((part[2] << 24) | ((part[1] & 255) << 16) | ((part[0] & 255) << 8)) >> 8
    codes = [p >> 8 for p in part] + [last]
    return [c.astype(jnp.float32) * down for c in codes]


def load_all(pairs_of, sem):
    copies = [pltpu.make_async_copy(src, dst, sem.at[n]) for n, (src, dst) in enumerate(pairs_of)]
    for c in copies:
        c.start()
    for c in copies:
        c.wait()


def pack_kernel(right_ref, left_ref, right_words, left_words):
    pack_into(right_ref[...], right_words)
    pack_into(left_ref[...], left_words)


def solve_kernel(rows, pairs, where_ref, rank_ref, *refs):
    inverse, held, other = refs[:rows], refs[rows : rows + pairs], refs[rows + pairs : rows + 2 * pairs]
    out_ref, packed_ref, whole, right, sem = refs[rows + 2 * pairs :]
    floor, me = where_ref[0], where_ref[1]
    part = inverse[0].shape[0]
    words, cap = held[0].shape
    chunk = (words - 8) // 3 * 4
    quarters = pairs
    half, quarter = me // quarters, me % quarters
    moves = [
        (inverse[d], whole.at[pl.ds(pl.multiple_of((floor ^ d) * part, part), part), :]) for d in range(rows)
    ]
    for at in range(2 * pairs):
        moves.append(((held if at % 2 == 0 else other)[at // 2], right.at[at]))
    load_all(moves, sem)
    column = lax.broadcasted_iota(jnp.int32, (1, cap), 1)
    for h in range(2):
        total = None
        for d in range(quarters):
            lhs = whole[:, pl.ds(pl.multiple_of((quarter ^ d) * chunk, chunk), chunk)]
            planes, scale = byte_planes(right[h * quarters + d])
            term = 0.0
            for plane in planes:
                term = term * 256.0 + jnp.dot(lhs, plane, preferred_element_type=jnp.float32)
            term = term * scale
            total = term if total is None else total + term
        tile = half ^ h
        kept = column < rank_ref[tile]
        out_ref[:, pl.ds(pl.multiple_of(tile * cap, cap), cap)] = jnp.where(kept, total, 0.0)
    pack_into(out_ref[...], packed_ref)


def core_kernel(rows, pairs, where_ref, own_ref, *refs):
    blocks = refs[: 2 * rows - 1]
    own_out, packed_out, (words, sem) = refs[2 * rows - 1], refs[2 * rows : -2], refs[-2:]
    floor, me = where_ref[0], where_ref[1]
    pair, side = me // 2, me % 2
    cap = own_out.shape[1]
    load_all([(ref, words.at[n]) for n, ref in enumerate(blocks)], sem)
    mine = pl.ds(pl.multiple_of(side * cap, cap), cap)

    def halves(x):
        high = x.astype(jnp.bfloat16)
        return high, (x - high.astype(jnp.float32)).astype(jnp.bfloat16)

    left = jnp.concatenate([own_ref[...], *unpack(words[rows - 1])], axis=0)
    left_high, left_low = [x.T for x in halves(left)]
    for e in range(pairs):
        wanted = floor ^ pair ^ e
        near = jnp.concatenate(unpack(words[jnp.maximum(wanted, 1) - 1, :, mine]), axis=0)
        near = jnp.where(wanted == 0, own_ref[:, mine], near)
        high, low = halves(jnp.concatenate([near, *unpack(words[rows - 1 + wanted, :, mine])], axis=0))
        part = jnp.dot(left_high, high, preferred_element_type=jnp.float32)
        part += jnp.dot(left_high, low, preferred_element_type=jnp.float32)
        part += jnp.dot(left_low, high, preferred_element_type=jnp.float32)
        if e == 0:
            own_out[...] = part
        else:
            pack_into(part, packed_out[e - 1])


def choose_kernel(rows, pairs, where_ref, *refs):
    ins, outs = refs[:rows], refs[rows:]
    mark = where_ref[0] ^ (where_ref[1] // 2)
    for e in range(pairs):
        for d in range(rows):

            @pl.when(mark == d ^ e)
            def _(d=d, e=e):
                outs[e][...] = ins[d][...]


def put_pieces(values, slot, count, pieces, whole=None):
    piece, cap = values[0].shape
    for i in range(4):
        at = pl.ds(pl.multiple_of(slot * (4 * piece) + piece * i, piece), piece)
        if whole is not None:
            whole[at, :] = values[i]
        for n, value in enumerate(split_three(values[i])[:count]):
            pieces[at, n * cap : (n + 1) * cap] = value


def row_kernel(pairs, where_ref, *refs):
    blocks, (out_ref, words, sem) = refs[: 2 * pairs], refs[2 * pairs :]
    load_all([(ref, words.at[n]) for n, ref in enumerate(blocks)], sem)
    for n in range(2 * pairs):
        put_pieces(unpack(words[n]), where_ref[1] ^ (2 * (n % pairs) + n // pairs), 3, out_ref)


def column_kernel(pairs, where_ref, *refs):
    blocks, (whole_ref, out_ref, words, sem) = refs[: 2 * pairs], refs[2 * pairs :]
    me = where_ref[1]
    pair, side = me // 2, me % 2
    half = pairs // 2
    load_all([(ref, words.at[n]) for n, ref in enumerate(blocks)], sem)
    upper = (pair // half) ^ side
    for n in range(pairs):
        e = n % half + half * upper
        from_other = n // half
        slot = 2 * ((pair ^ e) % half) + (side ^ from_other)
        put_pieces(unpack(words[from_other * pairs + e]), slot, 2, out_ref, whole_ref)


def stacked(pieces, picks):
    return jnp.concatenate([pieces[n] for n in picks], axis=0)


def wide_six(lhs, right):
    cap = right.shape[0]
    r = split_three(right)
    total = jnp.dot(lhs, stacked(r, (0, 0, 0)), preferred_element_type=jnp.float32)
    total += jnp.dot(lhs[:, : 2 * cap], stacked(r, (1, 1)), preferred_element_type=jnp.float32)
    return total + jnp.dot(lhs[:, :cap], r[2], preferred_element_type=jnp.float32)


def wide_three(lhs, right):
    cap = right.shape[0]
    r = split_three(right)
    total = jnp.dot(lhs, stacked(r, (0, 0)), preferred_element_type=jnp.float32)
    return total + jnp.dot(lhs[:, :cap], r[1], preferred_element_type=jnp.float32)


def over_rows(x, y):
    return lax.dot_general(x, y, (((0,), (0,)), ((), ())), preferred_element_type=jnp.float32)


def local_kernel(t, rank_ref, left_in, right_in, probe_in, part_ref, left_pieces, right_pieces, left, right, probe, sem):
    load_all([(left_in.at[t], left), (right_in.at[t], right), (probe_in.at[t], probe)], sem)
    order, cap = left.shape
    step = order // 4
    row = lax.broadcasted_iota(jnp.int32, (cap, cap), 0)
    column = lax.broadcasted_iota(jnp.int32, (cap, cap), 1)
    product = jnp.zeros((cap, cap), jnp.float32)
    for s in range(0, order, step):
        product += hot_dot(right[s : s + step], probe[s : s + step], ((0,), (0,)))
    rank = rank_ref[t, 0]
    product = jnp.where((row < rank) & (column < rank), product, 0.0) / order
    for s in range(0, order, step):
        at = slice(s, s + step)
        part_ref[at, :] = hot_dot(left[at], product, ((1,), (0,)))
        for ref, out in ((left, left_pieces), (right, right_pieces)):
            for n, value in enumerate(split_three(ref[at])[:2]):
                out[at, n * cap : (n + 1) * cap] = value


def final_kernel(parts, rank_ref, probe_ref, *refs):
    cores = refs[:parts]
    part, panel, left, right, col, sampled, basis, outs, inverse, scratch, sem, sem_out = refs[-12:]
    tiles, order, cap = part.shape
    tall = refs[parts : parts + 3 * tiles + 2]
    basis_out, factor_out = refs[parts + 3 * tiles + 2 : -12]
    step = order // 4
    loads = []
    moves = []
    for t in range(tiles):
        moves += [(tall[3 * t], part.at[t]), (tall[3 * tiles].at[t], panel.at[t])]
    for t in range(tiles):
        moves += [(tall[3 * t + 1], left.at[t]), (tall[3 * t + 2], right.at[t])]
    for src, dst in [*moves, (tall[3 * tiles + 1], col)]:
        loads.append(pltpu.make_async_copy(src, dst, sem.at[len(loads)]))
    for c in loads:
        c.start()
    root = math.sqrt(order)
    row = lax.broadcasted_iota(jnp.int32, (cap, cap), 0)
    column = lax.broadcasted_iota(jnp.int32, (cap, cap), 1)

    total = cores[0][...]
    for c in cores[1:]:
        total = total + jnp.concatenate(unpack(c[...]), axis=0)

    def core(t):
        return total[t * cap : (t + 1) * cap] / order

    grams = []
    for t in range(tiles):
        weight = hot_dot(core(t), probe_ref[t], ((1,), (0,))) / order
        loads[2 * t].wait()
        loads[2 * t + 1].wait()
        same = jnp.zeros((cap, cap), jnp.float32)
        cross = jnp.zeros((cap, cap), jnp.float32)
        for s in range(0, order, step):
            at = slice(s, s + step)
            value = part[t, at] - wide_six(panel[t, at], weight)
            pieces = split_three(value)
            for n in range(3):
                sampled[t, at, n * cap : (n + 1) * cap] = pieces[n]
            product = over_rows(pieces[0], sampled[t, at])
            same += product[:, :cap] + over_rows(pieces[1], pieces[1])
            cross += product[:, cap : 2 * cap] + product[:, 2 * cap :]
        gram = same + (cross + cross.T)
        grams.append(gram + jnp.where((row == column) & (column >= rank_ref[t, 0]), 1.0, 0.0))

    def put(t, lo, value):
        inverse[t, lo : lo + value.shape[0], :] = value

    inverse_factor(lambda t: grams[t], put, cap, 64, scratch, tiles)
    for c in loads[2 * tiles :]:
        c.wait()
    sends = []
    for t in range(tiles):
        weight = inverse[t].T * root
        left_proj = jnp.zeros((cap, cap), jnp.float32)
        panel_proj = jnp.zeros((cap, cap), jnp.float32)
        for s in range(0, order, step):
            at = slice(s, s + step)
            value = wide_six(sampled[t, at], weight)
            outs[t, at, :] = value
            high, low, _ = split_three(value)
            one = over_rows(high, left[t, at])
            left_proj += one[:, :cap] + one[:, cap:] + over_rows(low, left[t, at, :cap])
            one = over_rows(high, panel[t, at, : 2 * cap])
            panel_proj += one[:, :cap] + one[:, cap:] + over_rows(low, panel[t, at, :cap])
        sends.append(pltpu.make_async_copy(outs.at[t], basis_out.at[t], sem_out.at[t]))
        sends[-1].start()
        left_proj = jnp.where(column < rank_ref[t, 0], left_proj, 0.0).T / order
        core_proj = hot_dot(core(t), panel_proj, ((0,), (1,))) / order
        for s in range(0, order, step):
            at = slice(s, s + step)
            basis[t, at, :] = wide_three(right[t, at], left_proj) - wide_three(col[at], core_proj)
        sends.append(pltpu.make_async_copy(basis.at[t], factor_out.at[t], sem_out.at[tiles + t]))
        sends[-1].start()
    for c in sends:
        c.wait()


def make_shards(rows, cols):
    pairs = cols // 2

    def shards(factor_inverse, panel_left, panel_right, panel_rank, left, right, probes, trail_rank):
        tile_rows, tile_cols = trail_rank.shape
        tile_order = factor_inverse.shape[1]
        rank_cap = left.shape[1] // tile_cols
        chunk = panel_left.shape[0]
        part = factor_inverse.shape[0]
        me = lax.axis_index("col").astype(jnp.int32)
        floor = lax.axis_index("row").astype(jnp.int32)
        spot = jnp.stack([floor, me])
        columns = jnp.arange(rank_cap, dtype=jnp.int32)
        my_pair, my_side = me // 2, me % 2
        wide = tile_rows * rank_cap

        words_shape = (packed_rows(chunk), rank_cap)
        words_out = shaped(words_shape, jnp.int32)
        right_words, words = call(pack_kernel, [words_out] * 2, [panel_right, panel_left], "vvvv")
        inverse, rest = floor_gather(factor_inverse, rows)
        inverse = rest(inverse)
        held = [right_words] + [flip(right_words, "col", cols, 2 * e) for e in range(1, pairs)]

        tall = (tile_rows, tile_order, rank_cap)
        flat = (tile_order, rank_cap)
        locals_ = [
            call(
                functools.partial(local_kernel, t),
                [shaped(flat)] + [shaped((tile_order, 2 * rank_cap), jnp.bfloat16)] * 2,
                [trail_rank, left.reshape(tall), right.reshape(tall), probes.reshape(tall)],
                "saaavvv",
                [pltpu.VMEM(flat, jnp.float32)] * 3 + [pltpu.SemaphoreType.DMA((3,))],
                flops=24 * tile_order * rank_cap * rank_cap,
            )
            for t in range(tile_rows)
        ]
        held, inverse, words, locals_[0] = lax.optimization_barrier((held, inverse, words, locals_[0]))
        other = [flip(h, "col", cols, 1) for h in held]
        row_held = [words] + [flip(words, "col", cols, 2 * e) for e in range(1, pairs)]

        solved, solved_words = call(
            lambda *refs: solve_kernel(rows, pairs, *refs),
            [shaped((rows * part, wide)), shaped((packed_rows(rows * part), wide), jnp.int32)],
            [spot, panel_rank, *inverse, *held, *other],
            "ss" + "a" * (rows + 2 * pairs) + "vv",
            [
                pltpu.VMEM((rows * part, tile_order), jnp.bfloat16),
                pltpu.VMEM((cols, *words_shape), jnp.int32),
                pltpu.SemaphoreType.DMA((rows + cols,)),
            ],
            flops=6 * rows * part * tile_order * wide,
        )
        from_floors, rest_left = floor_gather(after(words, *other), rows)
        solved_words, row_held, from_floors = lax.optimization_barrier((solved_words, row_held, from_floors))
        from_floors = rest_left(from_floors)
        arrived, rest = floor_gather(solved_words, rows)
        arrived = rest(arrived)

        row_other = [flip(h, "col", cols, 1) for h in row_held]
        panel_pieces = call(
            lambda *refs: row_kernel(pairs, *refs),
            [shaped((cols * chunk, 3 * rank_cap), jnp.bfloat16)],
            [spot, *row_held, *row_other],
            "s" + "a" * (2 * pairs) + "v",
            [pltpu.VMEM((2 * pairs, *words_shape), jnp.int32), pltpu.SemaphoreType.DMA((2 * pairs,))],
        )[0]
        from_floors, _, panel_pieces, *locals_[1:] = lax.optimization_barrier(
            (from_floors, solved_words, panel_pieces, *locals_[1:])
        )
        mixed = call(
            lambda *refs: choose_kernel(rows, pairs, *refs),
            [words_out] * pairs,
            [spot, *from_floors],
            "s" + "v" * (rows + pairs),
        )
        mixed = [flip(mixed[e], "col", cols, 2 * e) if e else mixed[e] for e in range(pairs)]

        passed = [flip(a, "col", cols, 1) for a in arrived]
        arrived, passed, mixed = lax.optimization_barrier((arrived, passed, mixed))
        parts = call(
            lambda *refs: core_kernel(rows, pairs, *refs),
            [shaped((wide, rank_cap))] + [shaped((packed_rows(wide), rank_cap), jnp.int32)] * (pairs - 1),
            [spot, solved, *arrived[1:], *passed],
            "sv" + "a" * (2 * rows - 1) + "v" * pairs,
            [
                pltpu.VMEM((2 * rows - 1, *solved_words.shape), jnp.int32),
                pltpu.SemaphoreType.DMA((2 * rows - 1,)),
            ],
            flops=12 * rows * part * wide * rank_cap * pairs,
        )
        swapped = [flip(m, "col", cols, 1) for m in lax.optimization_barrier((mixed, parts))[0]]
        parts = [flip(parts[e], "col", cols, 2 * e) if e else parts[e] for e in range(pairs)]
        col_left, col_pieces = call(
            lambda *refs: column_kernel(pairs, *refs),
            [shaped(flat), shaped((tile_order, 2 * rank_cap), jnp.bfloat16)],
            [spot, *mixed, *swapped],
            "s" + "a" * (2 * pairs) + "vv",
            [pltpu.VMEM((2 * pairs, *words_shape), jnp.int32), pltpu.SemaphoreType.DMA((2 * pairs,))],
        )

        panel_probe = dot("nk,tnl->tkl", col_left, probes.reshape(tall))
        panel_probe = jnp.where(columns[None, None, :] < trail_rank[:, :, None], panel_probe, 0.0)
        parts, panel_probe = lax.optimization_barrier((parts, panel_probe))

        new_basis, new_factor = call(
            lambda *refs: final_kernel(pairs, *refs),
            [shaped(tall), shaped(tall)],
            [
                trail_rank,
                panel_probe,
                *parts,
                *[x for group in locals_ for x in group],
                panel_pieces.reshape(tile_rows, tile_order, 3 * rank_cap),
                col_pieces,
            ],
            "sv" + "v" * pairs + "a" * (3 * tile_rows + 4),
            [
                pltpu.VMEM(tall, jnp.float32),
                pltpu.VMEM((tile_rows, tile_order, 3 * rank_cap), jnp.bfloat16),
                pltpu.VMEM((tile_rows, tile_order, 2 * rank_cap), jnp.bfloat16),
                pltpu.VMEM((tile_rows, tile_order, 2 * rank_cap), jnp.bfloat16),
                pltpu.VMEM((tile_order, 2 * rank_cap), jnp.bfloat16),
                pltpu.VMEM((tile_rows, tile_order, 3 * rank_cap), jnp.bfloat16),
                pltpu.VMEM(tall, jnp.float32),
                pltpu.VMEM(tall, jnp.float32),
                pltpu.VMEM((tile_rows, rank_cap, rank_cap), jnp.float32),
                pltpu.VMEM((tile_rows, SUB + 1, SUB, 128), jnp.float32),
                pltpu.SemaphoreType.DMA((4 * tile_rows + 1,)),
                pltpu.SemaphoreType.DMA((2 * tile_rows,)),
            ],
            flops=60 * tile_rows * tile_order * rank_cap * rank_cap,
        )
        return (
            new_basis.reshape(tile_rows * tile_order, rank_cap),
            new_factor.reshape(tile_rows * tile_order, rank_cap),
        )

    return shards


def solution(mesh):
    return jax.shard_map(
        make_shards(mesh.shape["row"], mesh.shape["col"]),
        mesh=mesh,
        in_specs=(
            P(("row", "col"), None),
            P(("row", "col"), None),
            P(("row", "col"), None),
            P("row"),
            P("row", "col"),
            P("row", "col"),
            P("row", "col"),
            P("row", "col"),
        ),
        out_specs=(P("row", "col"), P("row", "col")),
        check_vma=False,
    )
```

```python
import functools
import math

import jax
import jax.numpy as jnp
from jax import lax
from jax.experimental import pallas as pl
from jax.experimental.pallas import tpu as pltpu
from jax.sharding import PartitionSpec as P

highest = lax.Precision.HIGHEST
SUB = 8


def split_three(x):
    a = x.astype(jnp.bfloat16)
    r = x - a.astype(jnp.float32)
    b = r.astype(jnp.bfloat16)
    c = (r - b.astype(jnp.float32)).astype(jnp.bfloat16)
    return a, b, c


def hot_dot(x, y, dims):
    return lax.dot_general(x, y, (dims, ((), ())), precision=lax.Precision.HIGHEST, preferred_element_type=jnp.float32)


def factor_blocks(block, scratch):
    count = len(block)
    n = block[0].shape[0]
    wide = 2 * n
    groups = n // SUB
    lane = lax.broadcasted_iota(jnp.int32, (SUB, wide), 1)
    sub = lax.broadcasted_iota(jnp.int32, (SUB, wide), 0)
    state = []
    for t in range(count):
        eye = [jnp.where(lane - n == sub + SUB * g, 1.0, 0.0) for g in range(groups)]
        full = jnp.concatenate([block[t], jnp.zeros((n, n), jnp.float32)], axis=1)
        state.append([full[SUB * g : SUB * (g + 1)] + eye[g] for g in range(groups)])
    out = [[None] * groups for _ in range(count)]
    for k in range(groups):
        for t in range(count):
            rows = state[t]
            spread = [
                [jnp.broadcast_to(rows[g][:, SUB * k + j : SUB * k + j + 1], (SUB, wide)) for j in range(SUB)]
                for g in range(k, groups)
            ]
            for j in range(SUB):
                scratch[t, j] = spread[0][j]
            scratch[t, SUB] = rows[k]
            a = [
                [jnp.broadcast_to(scratch[t, j, i : i + 1, :], (SUB, wide)) for j in range(i + 1)]
                for i in range(SUB)
            ]
            row = [jnp.broadcast_to(scratch[t, SUB, i : i + 1, :], (SUB, wide)) for i in range(SUB)]
            inv = [None] * SUB
            low = [[None] * SUB for _ in range(SUB)]
            for j in range(SUB):
                inv[j] = 1.0 / a[j][j]
                for i in range(j + 1, SUB):
                    low[i][j] = a[i][j] * inv[j]
                for i in range(j + 1, SUB):
                    for h in range(i, SUB):
                        a[h][i] = a[h][i] - low[h][j] * a[i][j]
                    row[i] = row[i] - low[i][j] * row[j]
            done = row[0] * lax.rsqrt(a[0][0])
            for i in range(1, SUB):
                done = jnp.where(sub == i, row[i] * lax.rsqrt(a[i][i]), done)
            out[t][k] = done
            for g in range(k + 1, groups):
                cols = spread[g - k]
                scaled = []
                value = rows[g]
                for j in range(SUB):
                    x = cols[j]
                    for h in range(j):
                        x = x - scaled[h] * a[j][h]
                    scaled.append(x * inv[j])
                    value = value - scaled[j] * row[j]
                rows[g] = value
    return [jnp.concatenate(o, axis=0)[:, n:] for o in out]


def inverse_factor(gram_of, put, order, step, scratch, count):
    work = [gram_of(t) for t in range(count)]
    eye = (
        lax.broadcasted_iota(jnp.int32, (order, order), 0) == lax.broadcasted_iota(jnp.int32, (order, order), 1)
    )
    scale = []
    for t in range(count):
        diag = jnp.where(eye, work[t], 0.0)
        down = lax.rsqrt(jnp.sum(diag, axis=1, keepdims=True))
        across = lax.rsqrt(jnp.sum(diag, axis=0, keepdims=True))
        scale.append(across)
        work[t] = jnp.concatenate([work[t] * down * across, jnp.where(eye, 1.0, 0.0)], axis=1)
    for k in range(order // step):
        lo = k * step
        inner = factor_blocks([w[:step, lo : lo + step] for w in work], scratch)
        for t in range(count):
            solved = hot_dot(inner[t], work[t][:step], ((1,), (0,)))
            put(t, lo, solved[:, order:] * scale[t])
            if lo + step < order:
                tail = solved[:, lo + step : order]
                work[t] = work[t][step:] - hot_dot(tail, solved, ((0,), (0,)))


def flip(value, axis, size, mask):
    return lax.ppermute(value, axis, [(i, i ^ mask) for i in range(size)])


def floor_gather(block, size, gate=None):
    got = {0: block}
    got.update({d: flip(block, "row", size, d) for d in range(1, size) if d & (d - 1) == 0})
    for d in sorted(set(range(1, size)) - set(got), key=lambda d: (bin(d).count("1"), d)):
        source = got[d & (d - 1)]
        got[d] = flip(source if gate is None else after(source, gate), "row", size, d & -d)
    return [got[d] for d in range(size)]


def after(value, *earlier):
    return lax.optimization_barrier((value, *earlier))[0]


def dot(spec, a, b):
    return jnp.einsum(spec, a, b, precision=highest, preferred_element_type=jnp.float32)


def shaped(shape, dtype=jnp.float32):
    return jax.ShapeDtypeStruct(shape, dtype)


def call(kernel, out, args, kinds, scratch=(), limit=60, flops=0, moved=None):
    spaces = {"v": pltpu.VMEM, "s": pltpu.SMEM, "a": pl.ANY}
    if moved is None:
        moved = sum(a.size * a.dtype.itemsize for a in [*out, *args])
    return pl.pallas_call(
        kernel,
        out_shape=out,
        in_specs=[pl.BlockSpec(memory_space=spaces[k]) for k in kinds[: len(args)]],
        out_specs=[pl.BlockSpec(memory_space=spaces[k]) for k in kinds[len(args) :]],
        scratch_shapes=list(scratch),
        compiler_params=pltpu.CompilerParams(vmem_limit_bytes=limit * 1024 * 1024),
        cost_estimate=pl.CostEstimate(flops=flops, bytes_accessed=moved, transcendentals=0),
    )(*args)


def power_of_two(exponent):
    low = exponent + 128
    value = jnp.full(exponent.shape, 2.0**-64, jnp.float32)
    for bit in range(7):
        value = value * jnp.where((low >> bit) & 1 == 1, 2.0 ** (2**bit), 1.0)
    return value * jnp.where(low >= 128, 1.0, 2.0**-64) * jnp.where(low >= 128, 2.0**64, 1.0)


def packed_rows(rows):
    return rows // 4 * 3 + 8


def pack_into(value, out_ref):
    rows, width = value.shape
    piece = rows // 4
    top = jnp.max(jnp.abs(value), axis=0, keepdims=True)
    level = jnp.log(jnp.maximum(top, 2.0**-90)) * 1.4426950408889634
    exponent = jnp.floor(level).astype(jnp.int32) + 1
    factor_up = power_of_two(23 - exponent)
    limit = 2.0**23 - 1
    codes = [
        jnp.clip(jnp.round(value[piece * n : piece * (n + 1)] * factor_up), -limit, limit).astype(jnp.int32)
        for n in range(4)
    ]
    for n in range(3):
        out_ref[piece * n : piece * (n + 1), :] = (codes[n] << 8) | ((codes[3] >> (8 * n)) & 255)
    out_ref[3 * piece :, :] = jnp.broadcast_to(exponent, (8, width))


def byte_planes(words):
    piece = (words.shape[0] - 8) // 3
    part = [words[piece * n : piece * (n + 1)] for n in range(3)]
    planes = [
        [p >> 24 for p in part] + [(part[2] << 24) >> 24],
        [(p >> 16) & 255 for p in part] + [part[1] & 255],
        [(p >> 8) & 255 for p in part] + [part[0] & 255],
    ]
    whole = [jnp.concatenate([x.astype(jnp.float32) for x in p], axis=0).astype(jnp.bfloat16) for p in planes]
    return whole, power_of_two(words[3 * piece : 3 * piece + 1] - 23)


def unpack(words):
    rows, width = words.shape
    piece = (rows - 8) // 3
    part = [words[piece * n : piece * (n + 1)] for n in range(3)]
    down = power_of_two(words[3 * piece : 3 * piece + 1] - 23)
    last = ((part[2] << 24) | ((part[1] & 255) << 16) | ((part[0] & 255) << 8)) >> 8
    codes = [p >> 8 for p in part] + [last]
    return [c.astype(jnp.float32) * down for c in codes]


def load_all(pairs_of, sem):
    copies = [pltpu.make_async_copy(src, dst, sem.at[n]) for n, (src, dst) in enumerate(pairs_of)]
    for c in copies:
        c.start()
    for c in copies:
        c.wait()


def pack_kernel(right_ref, left_ref, both_ref, left_words_ref):
    pack_into(right_ref[...], both_ref.at[0])
    pack_into(left_ref[...], left_words_ref)
    both_ref[1] = left_words_ref[...]


def solve_kernel(rows, pairs, where_ref, rank_ref, *refs):
    inverse, held, other = refs[:rows], refs[rows : rows + pairs], refs[rows + pairs : rows + 2 * pairs]
    out_ref, packed_ref, whole, right, sem = refs[rows + 2 * pairs :]
    floor, me = where_ref[0], where_ref[1]
    part = inverse[0].shape[0]
    words, cap = held[0].shape[1:]
    chunk = (words - 8) // 3 * 4
    quarters = pairs
    half, quarter = me // quarters, me % quarters
    moves = [
        (inverse[d], whole.at[pl.ds(pl.multiple_of((floor ^ d) * part, part), part), :]) for d in range(rows)
    ]
    for at in range(2 * pairs):
        moves.append(((held if at % 2 == 0 else other)[at // 2].at[0], right.at[at]))
    load_all(moves, sem)
    column = lax.broadcasted_iota(jnp.int32, (1, cap), 1)
    for h in range(2):
        total = None
        for d in range(quarters):
            lhs = whole[:, pl.ds(pl.multiple_of((quarter ^ d) * chunk, chunk), chunk)]
            planes, scale = byte_planes(right[h * quarters + d])
            term = 0.0
            for plane in planes:
                term = term * 256.0 + jnp.dot(lhs, plane, preferred_element_type=jnp.float32)
            term = term * scale
            total = term if total is None else total + term
        tile = half ^ h
        kept = column < rank_ref[tile]
        out_ref[:, pl.ds(pl.multiple_of(tile * cap, cap), cap)] = jnp.where(kept, total, 0.0)
    pack_into(out_ref[...], packed_ref)


def core_kernel(rows, pairs, where_ref, own_ref, *refs):
    blocks = refs[: 2 * rows - 1]
    own_out, packed_out, (words, sem) = refs[2 * rows - 1], refs[2 * rows : -2], refs[-2:]
    floor, me = where_ref[0], where_ref[1]
    pair, side = me // 2, me % 2
    cap = own_out.shape[1]
    load_all([(ref, words.at[n]) for n, ref in enumerate(blocks)], sem)
    mine = pl.ds(pl.multiple_of(side * cap, cap), cap)

    def halves(x):
        high = x.astype(jnp.bfloat16)
        return high, (x - high.astype(jnp.float32)).astype(jnp.bfloat16)

    left = jnp.concatenate([own_ref[...], *unpack(words[rows - 1])], axis=0)
    left_high, left_low = [x.T for x in halves(left)]
    for e in range(pairs):
        wanted = floor ^ pair ^ e
        near = jnp.concatenate(unpack(words[jnp.maximum(wanted, 1) - 1, :, mine]), axis=0)
        near = jnp.where(wanted == 0, own_ref[:, mine], near)
        high, low = halves(jnp.concatenate([near, *unpack(words[rows - 1 + wanted, :, mine])], axis=0))
        part = jnp.dot(left_high, high, preferred_element_type=jnp.float32)
        part += jnp.dot(left_high, low, preferred_element_type=jnp.float32)
        part += jnp.dot(left_low, high, preferred_element_type=jnp.float32)
        if e == 0:
            own_out[...] = part
        else:
            pack_into(part, packed_out[e - 1])


def choose_kernel(rows, pairs, where_ref, *refs):
    ins, outs = refs[:rows], refs[rows:]
    mark = where_ref[0] ^ (where_ref[1] // 2)
    for e in range(pairs):
        for d in range(rows):

            @pl.when(mark == d ^ e)
            def _(d=d, e=e):
                outs[e][...] = ins[d][...]


def put_pieces(values, slot, count, pieces, whole=None):
    piece, cap = values[0].shape
    for i in range(4):
        at = pl.ds(pl.multiple_of(slot * (4 * piece) + piece * i, piece), piece)
        if whole is not None:
            whole[at, :] = values[i]
        for n, value in enumerate(split_three(values[i])[:count]):
            pieces[at, n * cap : (n + 1) * cap] = value


def row_kernel(pairs, where_ref, *refs):
    blocks, (out_ref, words, sem) = refs[: 2 * pairs], refs[2 * pairs :]
    load_all([(ref.at[1], words.at[n]) for n, ref in enumerate(blocks)], sem)
    for n in range(2 * pairs):
        put_pieces(unpack(words[n]), where_ref[1] ^ (2 * (n % pairs) + n // pairs), 3, out_ref)


def column_kernel(pairs, where_ref, *refs):
    blocks, (whole_ref, out_ref, words, sem) = refs[: 2 * pairs], refs[2 * pairs :]
    me = where_ref[1]
    pair, side = me // 2, me % 2
    half = pairs // 2
    load_all([(ref, words.at[n]) for n, ref in enumerate(blocks)], sem)
    upper = (pair // half) ^ side
    for n in range(pairs):
        e = n % half + half * upper
        from_other = n // half
        slot = 2 * ((pair ^ e) % half) + (side ^ from_other)
        put_pieces(unpack(words[from_other * pairs + e]), slot, 2, out_ref, whole_ref)


def stacked(pieces, picks):
    return jnp.concatenate([pieces[n] for n in picks], axis=0)


def wide_six(lhs, right):
    cap = right.shape[0]
    r = split_three(right)
    total = jnp.dot(lhs, stacked(r, (0, 0, 0)), preferred_element_type=jnp.float32)
    total += jnp.dot(lhs[:, : 2 * cap], stacked(r, (1, 1)), preferred_element_type=jnp.float32)
    return total + jnp.dot(lhs[:, :cap], r[2], preferred_element_type=jnp.float32)


def wide_three(lhs, right):
    cap = right.shape[0]
    r = split_three(right)
    total = jnp.dot(lhs, stacked(r, (0, 0)), preferred_element_type=jnp.float32)
    return total + jnp.dot(lhs[:, :cap], r[1], preferred_element_type=jnp.float32)


def over_rows(x, y):
    return lax.dot_general(x, y, (((0,), (0,)), ((), ())), preferred_element_type=jnp.float32)


def local_kernel(t, rank_ref, left_in, right_in, probe_in, part_ref, left_pieces, right_pieces, left, right, probe, sem):
    load_all([(left_in.at[t], left), (right_in.at[t], right), (probe_in.at[t], probe)], sem)
    order, cap = left.shape
    step = order // 4
    row = lax.broadcasted_iota(jnp.int32, (cap, cap), 0)
    column = lax.broadcasted_iota(jnp.int32, (cap, cap), 1)
    product = jnp.zeros((cap, cap), jnp.float32)
    for s in range(0, order, step):
        product += hot_dot(right[s : s + step], probe[s : s + step], ((0,), (0,)))
    rank = rank_ref[t, 0]
    product = jnp.where((row < rank) & (column < rank), product, 0.0) / order
    for s in range(0, order, step):
        at = slice(s, s + step)
        part_ref[at, :] = hot_dot(left[at], product, ((1,), (0,)))
        for ref, out in ((left, left_pieces), (right, right_pieces)):
            for n, value in enumerate(split_three(ref[at])[:2]):
                out[at, n * cap : (n + 1) * cap] = value


def final_kernel(parts, rank_ref, probe_ref, *refs):
    cores = refs[:parts]
    part, panel, left, right, col, sampled, basis, outs, inverse, scratch, sem, sem_out = refs[-12:]
    tiles, order, cap = part.shape
    tall = refs[parts : parts + 3 * tiles + 2]
    basis_out, factor_out = refs[parts + 3 * tiles + 2 : -12]
    step = order // 4
    loads = []
    moves = []
    for t in range(tiles):
        moves += [(tall[3 * t], part.at[t]), (tall[3 * tiles].at[t], panel.at[t])]
    for t in range(tiles):
        moves += [(tall[3 * t + 1], left.at[t]), (tall[3 * t + 2], right.at[t])]
    for src, dst in [*moves, (tall[3 * tiles + 1], col)]:
        loads.append(pltpu.make_async_copy(src, dst, sem.at[len(loads)]))
    for c in loads:
        c.start()
    root = math.sqrt(order)
    row = lax.broadcasted_iota(jnp.int32, (cap, cap), 0)
    column = lax.broadcasted_iota(jnp.int32, (cap, cap), 1)

    total = cores[0][...]
    for c in cores[1:]:
        total = total + jnp.concatenate(unpack(c[...]), axis=0)

    def core(t):
        return total[t * cap : (t + 1) * cap] / order

    grams = []
    for t in range(tiles):
        weight = hot_dot(core(t), probe_ref[t], ((1,), (0,))) / order
        loads[2 * t].wait()
        loads[2 * t + 1].wait()
        same = jnp.zeros((cap, cap), jnp.float32)
        cross = jnp.zeros((cap, cap), jnp.float32)
        for s in range(0, order, step):
            at = slice(s, s + step)
            value = part[t, at] - wide_six(panel[t, at], weight)
            pieces = split_three(value)
            for n in range(3):
                sampled[t, at, n * cap : (n + 1) * cap] = pieces[n]
            product = over_rows(pieces[0], sampled[t, at])
            same += product[:, :cap] + over_rows(pieces[1], pieces[1])
            cross += product[:, cap : 2 * cap] + product[:, 2 * cap :]
        gram = same + (cross + cross.T)
        grams.append(gram + jnp.where((row == column) & (column >= rank_ref[t, 0]), 1.0, 0.0))

    def put(t, lo, value):
        inverse[t, lo : lo + value.shape[0], :] = value

    inverse_factor(lambda t: grams[t], put, cap, 64, scratch, tiles)
    for c in loads[2 * tiles :]:
        c.wait()
    sends = []
    for t in range(tiles):
        weight = inverse[t].T * root
        left_proj = jnp.zeros((cap, cap), jnp.float32)
        panel_proj = jnp.zeros((cap, cap), jnp.float32)
        for s in range(0, order, step):
            at = slice(s, s + step)
            value = wide_six(sampled[t, at], weight)
            outs[t, at, :] = value
            high, low, _ = split_three(value)
            one = over_rows(high, left[t, at])
            left_proj += one[:, :cap] + one[:, cap:] + over_rows(low, left[t, at, :cap])
            one = over_rows(high, panel[t, at, : 2 * cap])
            panel_proj += one[:, :cap] + one[:, cap:] + over_rows(low, panel[t, at, :cap])
        sends.append(pltpu.make_async_copy(outs.at[t], basis_out.at[t], sem_out.at[t]))
        sends[-1].start()
        left_proj = jnp.where(column < rank_ref[t, 0], left_proj, 0.0).T / order
        core_proj = hot_dot(core(t), panel_proj, ((0,), (1,))) / order
        for s in range(0, order, step):
            at = slice(s, s + step)
            basis[t, at, :] = wide_three(right[t, at], left_proj) - wide_three(col[at], core_proj)
        sends.append(pltpu.make_async_copy(basis.at[t], factor_out.at[t], sem_out.at[tiles + t]))
        sends[-1].start()
    for c in sends:
        c.wait()


def make_shards(rows, cols):
    pairs = cols // 2

    def shards(factor_inverse, panel_left, panel_right, panel_rank, left, right, probes, trail_rank):
        tile_rows, tile_cols = trail_rank.shape
        tile_order = factor_inverse.shape[1]
        rank_cap = left.shape[1] // tile_cols
        chunk = panel_left.shape[0]
        part = factor_inverse.shape[0]
        me = lax.axis_index("col").astype(jnp.int32)
        floor = lax.axis_index("row").astype(jnp.int32)
        spot = jnp.stack([floor, me])
        columns = jnp.arange(rank_cap, dtype=jnp.int32)
        my_pair, my_side = me // 2, me % 2
        wide = tile_rows * rank_cap

        words_shape = (packed_rows(chunk), rank_cap)
        words_out = shaped(words_shape, jnp.int32)
        both, words = call(
            pack_kernel, [shaped((2, *words_shape), jnp.int32), words_out], [panel_right, panel_left], "vvvv"
        )
        inverse = floor_gather(factor_inverse, rows)
        words = after(words, *inverse[1:])
        held = [both] + [flip(both, "col", cols, 2 * e) for e in range(1, pairs)]
        from_floors = floor_gather(words, rows)
        first = [d for d in range(rows) if d & (d - 1) == 0]

        tall = (tile_rows, tile_order, rank_cap)
        flat = (tile_order, rank_cap)

        def local(t, rank):
            return call(
                functools.partial(local_kernel, t),
                [shaped(flat)] + [shaped((tile_order, 2 * rank_cap), jnp.bfloat16)] * 2,
                [rank, left.reshape(tall), right.reshape(tall), probes.reshape(tall)],
                "saaavvv",
                [pltpu.VMEM(flat, jnp.float32)] * 3 + [pltpu.SemaphoreType.DMA((3,))],
                moved=0,
            )

        locals_ = [local(0, after(trail_rank, inverse[-1]))]
        held, inverse, locals_, _ = lax.optimization_barrier(
            (held, inverse, locals_, [from_floors[d] for d in first])
        )
        other = [flip(h, "col", cols, 1) for h in held]
        other, from_floors = lax.optimization_barrier((other, from_floors))

        solved, solved_words = call(
            lambda *refs: solve_kernel(rows, pairs, *refs),
            [shaped((rows * part, wide)), shaped((packed_rows(rows * part), wide), jnp.int32)],
            [spot, panel_rank, *inverse, *held, *other],
            "ss" + "a" * (rows + 2 * pairs) + "vv",
            [
                pltpu.VMEM((rows * part, tile_order), jnp.bfloat16),
                pltpu.VMEM((cols, *words_shape), jnp.int32),
                pltpu.SemaphoreType.DMA((rows + cols,)),
            ],
            flops=6 * rows * part * tile_order * wide,
        )
        from_floors, _ = lax.optimization_barrier((from_floors, solved_words))
        mixed = call(
            lambda *refs: choose_kernel(rows, pairs, *refs),
            [words_out] * pairs,
            [spot, *from_floors],
            "s" + "v" * (rows + pairs),
        )
        panel_pieces = call(
            lambda *refs: row_kernel(pairs, *refs),
            [shaped((cols * chunk, 3 * rank_cap), jnp.bfloat16)],
            [after(spot, solved_words), *held, *other],
            "s" + "a" * (2 * pairs) + "v",
            [pltpu.VMEM((2 * pairs, *words_shape), jnp.int32), pltpu.SemaphoreType.DMA((2 * pairs,))],
            moved=0,
        )[0]
        locals_ += [local(t, after(trail_rank, mixed[0])) for t in range(1, tile_rows)]
        mixed = [flip(mixed[e], "col", cols, 2 * e) if e else mixed[e] for e in range(pairs)]
        arrived = floor_gather(solved_words, rows, (locals_[-1], mixed[1:]))

        arrived, mixed, panel_pieces, locals_ = lax.optimization_barrier((arrived, mixed, panel_pieces, locals_))
        passed = [flip(a, "col", cols, 1) for a in arrived]
        parts = call(
            lambda *refs: core_kernel(rows, pairs, *refs),
            [shaped((wide, rank_cap))] + [shaped((packed_rows(wide), rank_cap), jnp.int32)] * (pairs - 1),
            [spot, solved, *arrived[1:], *passed],
            "sv" + "a" * (2 * rows - 1) + "v" * pairs,
            [
                pltpu.VMEM((2 * rows - 1, *solved_words.shape), jnp.int32),
                pltpu.SemaphoreType.DMA((2 * rows - 1,)),
            ],
            flops=12 * rows * part * wide * rank_cap * pairs,
        )
        swapped = [flip(m, "col", cols, 1) for m in lax.optimization_barrier((mixed, parts))[0]]
        parts = [flip(parts[e], "col", cols, 2 * e) if e else parts[e] for e in range(pairs)]
        col_left, col_pieces = call(
            lambda *refs: column_kernel(pairs, *refs),
            [shaped(flat), shaped((tile_order, 2 * rank_cap), jnp.bfloat16)],
            [spot, *mixed, *swapped],
            "s" + "a" * (2 * pairs) + "vv",
            [pltpu.VMEM((2 * pairs, *words_shape), jnp.int32), pltpu.SemaphoreType.DMA((2 * pairs,))],
        )

        panel_probe = dot("nk,tnl->tkl", col_left, probes.reshape(tall))
        panel_probe = jnp.where(columns[None, None, :] < trail_rank[:, :, None], panel_probe, 0.0)
        parts, panel_probe = lax.optimization_barrier((parts, panel_probe))

        new_basis, new_factor = call(
            lambda *refs: final_kernel(pairs, *refs),
            [shaped(tall), shaped(tall)],
            [
                trail_rank,
                panel_probe,
                *parts,
                *[x for group in locals_ for x in group],
                panel_pieces.reshape(tile_rows, tile_order, 3 * rank_cap),
                col_pieces,
            ],
            "sv" + "v" * pairs + "a" * (3 * tile_rows + 4),
            [
                pltpu.VMEM(tall, jnp.float32),
                pltpu.VMEM((tile_rows, tile_order, 3 * rank_cap), jnp.bfloat16),
                pltpu.VMEM((tile_rows, tile_order, 2 * rank_cap), jnp.bfloat16),
                pltpu.VMEM((tile_rows, tile_order, 2 * rank_cap), jnp.bfloat16),
                pltpu.VMEM((tile_order, 2 * rank_cap), jnp.bfloat16),
                pltpu.VMEM((tile_rows, tile_order, 3 * rank_cap), jnp.bfloat16),
                pltpu.VMEM(tall, jnp.float32),
                pltpu.VMEM(tall, jnp.float32),
                pltpu.VMEM((tile_rows, rank_cap, rank_cap), jnp.float32),
                pltpu.VMEM((tile_rows, SUB + 1, SUB, 128), jnp.float32),
                pltpu.SemaphoreType.DMA((4 * tile_rows + 1,)),
                pltpu.SemaphoreType.DMA((2 * tile_rows,)),
            ],
            flops=60 * tile_rows * tile_order * rank_cap * rank_cap,
        )
        return (
            new_basis.reshape(tile_rows * tile_order, rank_cap),
            new_factor.reshape(tile_rows * tile_order, rank_cap),
        )

    return shards


def solution(mesh):
    return jax.shard_map(
        make_shards(mesh.shape["row"], mesh.shape["col"]),
        mesh=mesh,
        in_specs=(
            P(("row", "col"), None),
            P(("row", "col"), None),
            P(("row", "col"), None),
            P("row"),
            P("row", "col"),
            P("row", "col"),
            P("row", "col"),
            P("row", "col"),
        ),
        out_specs=(P("row", "col"), P("row", "col")),
        check_vma=False,
    )
```

```python
import functools
import math

import jax
import jax.numpy as jnp
from jax import lax
from jax.experimental import pallas as pl
from jax.experimental.pallas import tpu as pltpu
from jax.sharding import PartitionSpec as P

highest = lax.Precision.HIGHEST
SUB = 8


def split_three(x):
    a = x.astype(jnp.bfloat16)
    r = x - a.astype(jnp.float32)
    b = r.astype(jnp.bfloat16)
    c = (r - b.astype(jnp.float32)).astype(jnp.bfloat16)
    return a, b, c


def hot_dot(x, y, dims):
    return lax.dot_general(x, y, (dims, ((), ())), precision=lax.Precision.HIGHEST, preferred_element_type=jnp.float32)


def factor_blocks(block, scratch):
    count = len(block)
    n = block[0].shape[0]
    wide = 2 * n
    groups = n // SUB
    lane = lax.broadcasted_iota(jnp.int32, (SUB, wide), 1)
    sub = lax.broadcasted_iota(jnp.int32, (SUB, wide), 0)
    state = []
    for t in range(count):
        eye = [jnp.where(lane - n == sub + SUB * g, 1.0, 0.0) for g in range(groups)]
        full = jnp.concatenate([block[t], jnp.zeros((n, n), jnp.float32)], axis=1)
        state.append([full[SUB * g : SUB * (g + 1)] + eye[g] for g in range(groups)])
    out = [[None] * groups for _ in range(count)]
    for k in range(groups):
        for t in range(count):
            rows = state[t]
            spread = [
                [jnp.broadcast_to(rows[g][:, SUB * k + j : SUB * k + j + 1], (SUB, wide)) for j in range(SUB)]
                for g in range(k, groups)
            ]
            for j in range(SUB):
                scratch[t, j] = spread[0][j]
            scratch[t, SUB] = rows[k]
            a = [
                [jnp.broadcast_to(scratch[t, j, i : i + 1, :], (SUB, wide)) for j in range(i + 1)]
                for i in range(SUB)
            ]
            row = [jnp.broadcast_to(scratch[t, SUB, i : i + 1, :], (SUB, wide)) for i in range(SUB)]
            inv = [None] * SUB
            low = [[None] * SUB for _ in range(SUB)]
            for j in range(SUB):
                inv[j] = 1.0 / a[j][j]
                for i in range(j + 1, SUB):
                    low[i][j] = a[i][j] * inv[j]
                for i in range(j + 1, SUB):
                    for h in range(i, SUB):
                        a[h][i] = a[h][i] - low[h][j] * a[i][j]
                    row[i] = row[i] - low[i][j] * row[j]
            done = row[0] * lax.rsqrt(a[0][0])
            for i in range(1, SUB):
                done = jnp.where(sub == i, row[i] * lax.rsqrt(a[i][i]), done)
            out[t][k] = done
            for g in range(k + 1, groups):
                cols = spread[g - k]
                scaled = []
                value = rows[g]
                for j in range(SUB):
                    x = cols[j]
                    for h in range(j):
                        x = x - scaled[h] * a[j][h]
                    scaled.append(x * inv[j])
                    value = value - scaled[j] * row[j]
                rows[g] = value
    return [jnp.concatenate(o, axis=0)[:, n:] for o in out]


def inverse_factor(gram_of, put, order, step, scratch, count):
    work = [gram_of(t) for t in range(count)]
    eye = (
        lax.broadcasted_iota(jnp.int32, (order, order), 0) == lax.broadcasted_iota(jnp.int32, (order, order), 1)
    )
    scale = []
    for t in range(count):
        diag = jnp.where(eye, work[t], 0.0)
        down = lax.rsqrt(jnp.sum(diag, axis=1, keepdims=True))
        across = lax.rsqrt(jnp.sum(diag, axis=0, keepdims=True))
        scale.append(across)
        work[t] = jnp.concatenate([work[t] * down * across, jnp.where(eye, 1.0, 0.0)], axis=1)
    for k in range(order // step):
        lo = k * step
        inner = factor_blocks([w[:step, lo : lo + step] for w in work], scratch)
        for t in range(count):
            solved = hot_dot(inner[t], work[t][:step], ((1,), (0,)))
            put(t, lo, solved[:, order:] * scale[t])
            if lo + step < order:
                tail = solved[:, lo + step : order]
                work[t] = work[t][step:] - hot_dot(tail, solved, ((0,), (0,)))


def flip(value, axis, size, mask):
    return lax.ppermute(value, axis, [(i, i ^ mask) for i in range(size)])


def floor_gather(block, size, gate=None):
    got = {0: block}
    got.update({d: flip(block, "row", size, d) for d in range(1, size) if d & (d - 1) == 0})
    for d in sorted(set(range(1, size)) - set(got), key=lambda d: (bin(d).count("1"), d)):
        source = got[d & (d - 1)]
        got[d] = flip(source if gate is None else after(source, gate), "row", size, d & -d)
    return [got[d] for d in range(size)]


def after(value, *earlier):
    return lax.optimization_barrier((value, *earlier))[0]


def dot(spec, a, b):
    return jnp.einsum(spec, a, b, precision=highest, preferred_element_type=jnp.float32)


def shaped(shape, dtype=jnp.float32):
    return jax.ShapeDtypeStruct(shape, dtype)


def call(kernel, out, args, kinds, scratch=(), limit=60, flops=0, moved=None):
    spaces = {"v": pltpu.VMEM, "s": pltpu.SMEM, "a": pl.ANY}
    if moved is None:
        moved = sum(a.size * a.dtype.itemsize for a in [*out, *args])
    return pl.pallas_call(
        kernel,
        out_shape=out,
        in_specs=[pl.BlockSpec(memory_space=spaces[k]) for k in kinds[: len(args)]],
        out_specs=[pl.BlockSpec(memory_space=spaces[k]) for k in kinds[len(args) :]],
        scratch_shapes=list(scratch),
        compiler_params=pltpu.CompilerParams(vmem_limit_bytes=limit * 1024 * 1024),
        cost_estimate=pl.CostEstimate(flops=flops, bytes_accessed=moved, transcendentals=0),
    )(*args)


def power_of_two(exponent):
    low = exponent + 128
    value = jnp.full(exponent.shape, 2.0**-64, jnp.float32)
    for bit in range(7):
        value = value * jnp.where((low >> bit) & 1 == 1, 2.0 ** (2**bit), 1.0)
    return value * jnp.where(low >= 128, 1.0, 2.0**-64) * jnp.where(low >= 128, 2.0**64, 1.0)


def packed_rows(rows):
    return rows // 4 * 3 + 8


def pack_into(value, out_ref):
    rows, width = value.shape
    piece = rows // 4
    top = jnp.max(jnp.abs(value), axis=0, keepdims=True)
    level = jnp.log(jnp.maximum(top, 2.0**-90)) * 1.4426950408889634
    exponent = jnp.floor(level).astype(jnp.int32) + 1
    factor_up = power_of_two(23 - exponent)
    limit = 2.0**23 - 1
    codes = [
        jnp.clip(jnp.round(value[piece * n : piece * (n + 1)] * factor_up), -limit, limit).astype(jnp.int32)
        for n in range(4)
    ]
    for n in range(3):
        out_ref[piece * n : piece * (n + 1), :] = (codes[n] << 8) | ((codes[3] >> (8 * n)) & 255)
    out_ref[3 * piece :, :] = jnp.broadcast_to(exponent, (8, width))


def byte_planes(words):
    piece = (words.shape[0] - 8) // 3
    part = [words[piece * n : piece * (n + 1)] for n in range(3)]
    planes = [
        [p >> 24 for p in part] + [(part[2] << 24) >> 24],
        [(p >> 16) & 255 for p in part] + [part[1] & 255],
        [(p >> 8) & 255 for p in part] + [part[0] & 255],
    ]
    whole = [jnp.concatenate([x.astype(jnp.float32) for x in p], axis=0).astype(jnp.bfloat16) for p in planes]
    return whole, power_of_two(words[3 * piece : 3 * piece + 1] - 23)


def unpack(words):
    rows, width = words.shape
    piece = (rows - 8) // 3
    part = [words[piece * n : piece * (n + 1)] for n in range(3)]
    down = power_of_two(words[3 * piece : 3 * piece + 1] - 23)
    last = ((part[2] << 24) | ((part[1] & 255) << 16) | ((part[0] & 255) << 8)) >> 8
    codes = [p >> 8 for p in part] + [last]
    return [c.astype(jnp.float32) * down for c in codes]


def load_all(pairs_of, sem):
    copies = [pltpu.make_async_copy(src, dst, sem.at[n]) for n, (src, dst) in enumerate(pairs_of)]
    for c in copies:
        c.start()
    for c in copies:
        c.wait()


def pack_kernel(right_ref, left_ref, both_ref, left_words_ref):
    pack_into(right_ref[...], both_ref.at[0])
    pack_into(left_ref[...], left_words_ref)
    both_ref[1] = left_words_ref[...]


def solve_kernel(rows, pairs, where_ref, rank_ref, *refs):
    inverse, held, other = refs[:rows], refs[rows : rows + pairs], refs[rows + pairs : rows + 2 * pairs]
    out_ref, packed_ref, whole, right, sem = refs[rows + 2 * pairs :]
    floor, me = where_ref[0], where_ref[1]
    part = inverse[0].shape[0]
    words, cap = held[0].shape[1:]
    chunk = (words - 8) // 3 * 4
    quarters = pairs
    half, quarter = me // quarters, me % quarters
    moves = [
        (inverse[d], whole.at[pl.ds(pl.multiple_of((floor ^ d) * part, part), part), :]) for d in range(rows)
    ]
    for at in range(2 * pairs):
        moves.append(((held if at % 2 == 0 else other)[at // 2].at[0], right.at[at]))
    load_all(moves, sem)
    column = lax.broadcasted_iota(jnp.int32, (1, cap), 1)
    for h in range(2):
        total = None
        for d in range(quarters):
            lhs = whole[:, pl.ds(pl.multiple_of((quarter ^ d) * chunk, chunk), chunk)]
            planes, scale = byte_planes(right[h * quarters + d])
            term = 0.0
            for plane in planes:
                term = term * 256.0 + jnp.dot(lhs, plane, preferred_element_type=jnp.float32)
            term = term * scale
            total = term if total is None else total + term
        tile = half ^ h
        kept = column < rank_ref[tile]
        out_ref[:, pl.ds(pl.multiple_of(tile * cap, cap), cap)] = jnp.where(kept, total, 0.0)
    pack_into(out_ref[...], packed_ref)


def core_kernel(rows, pairs, where_ref, own_ref, *refs):
    blocks = refs[: 2 * rows - 1]
    own_out, packed_out, (words, sem) = refs[2 * rows - 1], refs[2 * rows : -2], refs[-2:]
    floor, me = where_ref[0], where_ref[1]
    pair, side = me // 2, me % 2
    cap = own_out.shape[1]
    load_all([(ref, words.at[n]) for n, ref in enumerate(blocks)], sem)
    mine = pl.ds(pl.multiple_of(side * cap, cap), cap)

    def halves(x):
        high = x.astype(jnp.bfloat16)
        return high, (x - high.astype(jnp.float32)).astype(jnp.bfloat16)

    left = jnp.concatenate([own_ref[...], *unpack(words[rows - 1])], axis=0)
    left_high, left_low = [x.T for x in halves(left)]
    for e in range(pairs):
        wanted = floor ^ pair ^ e
        near = jnp.concatenate(unpack(words[jnp.maximum(wanted, 1) - 1, :, mine]), axis=0)
        near = jnp.where(wanted == 0, own_ref[:, mine], near)
        high, low = halves(jnp.concatenate([near, *unpack(words[rows - 1 + wanted, :, mine])], axis=0))
        part = jnp.dot(left_high, high, preferred_element_type=jnp.float32)
        part += jnp.dot(left_high, low, preferred_element_type=jnp.float32)
        part += jnp.dot(left_low, high, preferred_element_type=jnp.float32)
        if e == 0:
            own_out[...] = part
        else:
            pack_into(part, packed_out[e - 1])


def choose_kernel(rows, pairs, where_ref, *refs):
    ins, outs = refs[:rows], refs[rows:]
    mark = where_ref[0] ^ (where_ref[1] // 2)
    for e in range(pairs):
        for d in range(rows):

            @pl.when(mark == d ^ e)
            def _(d=d, e=e):
                outs[e][...] = ins[d][...]


def put_pieces(values, slot, count, pieces, whole=None):
    piece, cap = values[0].shape
    for i in range(4):
        at = pl.ds(pl.multiple_of(slot * (4 * piece) + piece * i, piece), piece)
        if whole is not None:
            whole[at, :] = values[i]
        for n, value in enumerate(split_three(values[i])[:count]):
            pieces[at, n * cap : (n + 1) * cap] = value


def row_kernel(pairs, where_ref, *refs):
    blocks, (out_ref, words, sem) = refs[: 2 * pairs], refs[2 * pairs :]
    load_all([(ref.at[1], words.at[n]) for n, ref in enumerate(blocks)], sem)
    for n in range(2 * pairs):
        put_pieces(unpack(words[n]), where_ref[1] ^ (2 * (n % pairs) + n // pairs), 3, out_ref)


def column_kernel(pairs, where_ref, *refs):
    blocks, (whole_ref, out_ref, words, sem) = refs[: 2 * pairs], refs[2 * pairs :]
    me = where_ref[1]
    pair, side = me // 2, me % 2
    half = pairs // 2
    load_all([(ref, words.at[n]) for n, ref in enumerate(blocks)], sem)
    upper = (pair // half) ^ side
    for n in range(pairs):
        e = n % half + half * upper
        from_other = n // half
        slot = 2 * ((pair ^ e) % half) + (side ^ from_other)
        put_pieces(unpack(words[from_other * pairs + e]), slot, 2, out_ref, whole_ref)


def stacked(pieces, picks):
    return jnp.concatenate([pieces[n] for n in picks], axis=0)


def wide_six(lhs, right):
    cap = right.shape[0]
    r = split_three(right)
    total = jnp.dot(lhs, stacked(r, (0, 0, 0)), preferred_element_type=jnp.float32)
    total += jnp.dot(lhs[:, : 2 * cap], stacked(r, (1, 1)), preferred_element_type=jnp.float32)
    return total + jnp.dot(lhs[:, :cap], r[2], preferred_element_type=jnp.float32)


def wide_three(lhs, right):
    cap = right.shape[0]
    r = split_three(right)
    total = jnp.dot(lhs, stacked(r, (0, 0)), preferred_element_type=jnp.float32)
    return total + jnp.dot(lhs[:, :cap], r[1], preferred_element_type=jnp.float32)


def over_rows(x, y):
    return lax.dot_general(x, y, (((0,), (0,)), ((), ())), preferred_element_type=jnp.float32)


def local_kernel(t, rank_ref, left_in, right_in, probe_in, part_ref, left_pieces, right_pieces, left, right, probe, sem):
    load_all([(left_in.at[t], left), (right_in.at[t], right), (probe_in.at[t], probe)], sem)
    order, cap = left.shape
    step = order // 4
    row = lax.broadcasted_iota(jnp.int32, (cap, cap), 0)
    column = lax.broadcasted_iota(jnp.int32, (cap, cap), 1)
    product = jnp.zeros((cap, cap), jnp.float32)
    for s in range(0, order, step):
        product += hot_dot(right[s : s + step], probe[s : s + step], ((0,), (0,)))
    rank = rank_ref[t, 0]
    product = jnp.where((row < rank) & (column < rank), product, 0.0) / order
    for s in range(0, order, step):
        at = slice(s, s + step)
        part_ref[at, :] = hot_dot(left[at], product, ((1,), (0,)))
        for ref, out in ((left, left_pieces), (right, right_pieces)):
            for n, value in enumerate(split_three(ref[at])[:2]):
                out[at, n * cap : (n + 1) * cap] = value


def final_kernel(parts, rank_ref, probe_ref, *refs):
    cores = refs[:parts]
    part, panel, left, right, col, sampled, basis, outs, inverse, scratch, sem, sem_out = refs[-12:]
    tiles, order, cap = part.shape
    tall = refs[parts : parts + 3 * tiles + 2]
    basis_out, factor_out = refs[parts + 3 * tiles + 2 : -12]
    step = order // 2
    loads = []
    moves = []
    for t in range(tiles):
        moves += [(tall[3 * t], part.at[t]), (tall[3 * tiles].at[t], panel.at[t])]
    for t in range(tiles):
        moves += [(tall[3 * t + 1], left.at[t]), (tall[3 * t + 2], right.at[t])]
    for src, dst in [*moves, (tall[3 * tiles + 1], col)]:
        loads.append(pltpu.make_async_copy(src, dst, sem.at[len(loads)]))
    for c in loads:
        c.start()
    root = math.sqrt(order)
    row = lax.broadcasted_iota(jnp.int32, (cap, cap), 0)
    column = lax.broadcasted_iota(jnp.int32, (cap, cap), 1)

    total = cores[0][...]
    for c in cores[1:]:
        total = total + jnp.concatenate(unpack(c[...]), axis=0)

    def core(t):
        return total[t * cap : (t + 1) * cap] / order

    grams = []
    for t in range(tiles):
        weight = hot_dot(core(t), probe_ref[t], ((1,), (0,))) / order
        loads[2 * t].wait()
        loads[2 * t + 1].wait()
        same = jnp.zeros((cap, cap), jnp.float32)
        cross = jnp.zeros((cap, cap), jnp.float32)
        for s in range(0, order, step):
            at = slice(s, s + step)
            value = part[t, at] - wide_six(panel[t, at], weight)
            pieces = split_three(value)
            for n in range(3):
                sampled[t, at, n * cap : (n + 1) * cap] = pieces[n]
            product = over_rows(pieces[0], sampled[t, at])
            same += product[:, :cap] + over_rows(pieces[1], pieces[1])
            cross += product[:, cap : 2 * cap] + product[:, 2 * cap :]
        gram = same + (cross + cross.T)
        grams.append(gram + jnp.where((row == column) & (column >= rank_ref[t, 0]), 1.0, 0.0))

    def put(t, lo, value):
        inverse[t, lo : lo + value.shape[0], :] = value

    inverse_factor(lambda t: grams[t], put, cap, 64, scratch, tiles)
    for c in loads[2 * tiles :]:
        c.wait()
    sends = []
    for t in range(tiles):
        weight = inverse[t].T * root
        left_proj = jnp.zeros((cap, cap), jnp.float32)
        panel_proj = jnp.zeros((cap, cap), jnp.float32)
        for s in range(0, order, step):
            at = slice(s, s + step)
            value = wide_six(sampled[t, at], weight)
            outs[t, at, :] = value
            high, low, _ = split_three(value)
            one = over_rows(high, left[t, at])
            left_proj += one[:, :cap] + one[:, cap:] + over_rows(low, left[t, at, :cap])
            one = over_rows(high, panel[t, at, : 2 * cap])
            panel_proj += one[:, :cap] + one[:, cap:] + over_rows(low, panel[t, at, :cap])
        sends.append(pltpu.make_async_copy(outs.at[t], basis_out.at[t], sem_out.at[t]))
        sends[-1].start()
        left_proj = jnp.where(column < rank_ref[t, 0], left_proj, 0.0).T / order
        core_proj = hot_dot(core(t), panel_proj, ((0,), (1,))) / order
        for s in range(0, order, step):
            at = slice(s, s + step)
            basis[t, at, :] = wide_three(right[t, at], left_proj) - wide_three(col[at], core_proj)
        sends.append(pltpu.make_async_copy(basis.at[t], factor_out.at[t], sem_out.at[tiles + t]))
        sends[-1].start()
    for c in sends:
        c.wait()


def make_shards(rows, cols):
    pairs = cols // 2

    def shards(factor_inverse, panel_left, panel_right, panel_rank, left, right, probes, trail_rank):
        tile_rows, tile_cols = trail_rank.shape
        tile_order = factor_inverse.shape[1]
        rank_cap = left.shape[1] // tile_cols
        chunk = panel_left.shape[0]
        part = factor_inverse.shape[0]
        me = lax.axis_index("col").astype(jnp.int32)
        floor = lax.axis_index("row").astype(jnp.int32)
        spot = jnp.stack([floor, me])
        columns = jnp.arange(rank_cap, dtype=jnp.int32)
        my_pair, my_side = me // 2, me % 2
        wide = tile_rows * rank_cap

        words_shape = (packed_rows(chunk), rank_cap)
        words_out = shaped(words_shape, jnp.int32)
        both, words = call(
            pack_kernel, [shaped((2, *words_shape), jnp.int32), words_out], [panel_right, panel_left], "vvvv"
        )
        inverse = floor_gather(factor_inverse, rows)
        words = after(words, *inverse[1:])
        held = [both] + [flip(both, "col", cols, 2 * e) for e in range(1, pairs)]
        from_floors = floor_gather(words, rows)
        first = [d for d in range(rows) if d & (d - 1) == 0]

        tall = (tile_rows, tile_order, rank_cap)
        flat = (tile_order, rank_cap)

        def local(t, rank):
            return call(
                functools.partial(local_kernel, t),
                [shaped(flat)] + [shaped((tile_order, 2 * rank_cap), jnp.bfloat16)] * 2,
                [rank, left.reshape(tall), right.reshape(tall), probes.reshape(tall)],
                "saaavvv",
                [pltpu.VMEM(flat, jnp.float32)] * 3 + [pltpu.SemaphoreType.DMA((3,))],
                moved=0,
            )

        locals_ = [local(0, after(trail_rank, inverse[-1]))]
        held, inverse, locals_, _ = lax.optimization_barrier(
            (held, inverse, locals_, [from_floors[d] for d in first])
        )
        other = [flip(h, "col", cols, 1) for h in held]
        other, from_floors = lax.optimization_barrier((other, from_floors))

        solved, solved_words = call(
            lambda *refs: solve_kernel(rows, pairs, *refs),
            [shaped((rows * part, wide)), shaped((packed_rows(rows * part), wide), jnp.int32)],
            [spot, panel_rank, *inverse, *held, *other],
            "ss" + "a" * (rows + 2 * pairs) + "vv",
            [
                pltpu.VMEM((rows * part, tile_order), jnp.bfloat16),
                pltpu.VMEM((cols, *words_shape), jnp.int32),
                pltpu.SemaphoreType.DMA((rows + cols,)),
            ],
            flops=6 * rows * part * tile_order * wide,
        )
        from_floors, _ = lax.optimization_barrier((from_floors, solved_words))
        mixed = call(
            lambda *refs: choose_kernel(rows, pairs, *refs),
            [words_out] * pairs,
            [spot, *from_floors],
            "s" + "v" * (rows + pairs),
        )
        panel_pieces = call(
            lambda *refs: row_kernel(pairs, *refs),
            [shaped((cols * chunk, 3 * rank_cap), jnp.bfloat16)],
            [after(spot, solved_words), *held, *other],
            "s" + "a" * (2 * pairs) + "v",
            [pltpu.VMEM((2 * pairs, *words_shape), jnp.int32), pltpu.SemaphoreType.DMA((2 * pairs,))],
            moved=0,
        )[0]
        locals_ += [local(t, after(trail_rank, mixed[0])) for t in range(1, tile_rows)]
        mixed = [flip(mixed[e], "col", cols, 2 * e) if e else mixed[e] for e in range(pairs)]
        arrived = floor_gather(solved_words, rows, (locals_[-1], mixed[1:]))

        passed = [flip(a, "col", cols, 1) for a in arrived[:-1]]
        arrived, passed, mixed, panel_pieces, locals_ = lax.optimization_barrier(
            (arrived, passed, mixed, panel_pieces, locals_)
        )
        passed.append(flip(arrived[-1], "col", cols, 1))
        parts = call(
            lambda *refs: core_kernel(rows, pairs, *refs),
            [shaped((wide, rank_cap))] + [shaped((packed_rows(wide), rank_cap), jnp.int32)] * (pairs - 1),
            [spot, solved, *arrived[1:], *passed],
            "sv" + "a" * (2 * rows - 1) + "v" * pairs,
            [
                pltpu.VMEM((2 * rows - 1, *solved_words.shape), jnp.int32),
                pltpu.SemaphoreType.DMA((2 * rows - 1,)),
            ],
            flops=12 * rows * part * wide * rank_cap * pairs,
        )
        swapped = [flip(m, "col", cols, 1) for m in lax.optimization_barrier((mixed, parts))[0]]
        parts = [flip(parts[e], "col", cols, 2 * e) if e else parts[e] for e in range(pairs)]
        col_left, col_pieces = call(
            lambda *refs: column_kernel(pairs, *refs),
            [shaped(flat), shaped((tile_order, 2 * rank_cap), jnp.bfloat16)],
            [spot, *mixed, *swapped],
            "s" + "a" * (2 * pairs) + "vv",
            [pltpu.VMEM((2 * pairs, *words_shape), jnp.int32), pltpu.SemaphoreType.DMA((2 * pairs,))],
        )

        panel_probe = dot("nk,tnl->tkl", col_left, probes.reshape(tall))
        panel_probe = jnp.where(columns[None, None, :] < trail_rank[:, :, None], panel_probe, 0.0)
        parts, panel_probe = lax.optimization_barrier((parts, panel_probe))

        new_basis, new_factor = call(
            lambda *refs: final_kernel(pairs, *refs),
            [shaped(tall), shaped(tall)],
            [
                trail_rank,
                panel_probe,
                *parts,
                *[x for group in locals_ for x in group],
                panel_pieces.reshape(tile_rows, tile_order, 3 * rank_cap),
                col_pieces,
            ],
            "sv" + "v" * pairs + "a" * (3 * tile_rows + 4),
            [
                pltpu.VMEM(tall, jnp.float32),
                pltpu.VMEM((tile_rows, tile_order, 3 * rank_cap), jnp.bfloat16),
                pltpu.VMEM((tile_rows, tile_order, 2 * rank_cap), jnp.bfloat16),
                pltpu.VMEM((tile_rows, tile_order, 2 * rank_cap), jnp.bfloat16),
                pltpu.VMEM((tile_order, 2 * rank_cap), jnp.bfloat16),
                pltpu.VMEM((tile_rows, tile_order, 3 * rank_cap), jnp.bfloat16),
                pltpu.VMEM(tall, jnp.float32),
                pltpu.VMEM(tall, jnp.float32),
                pltpu.VMEM((tile_rows, rank_cap, rank_cap), jnp.float32),
                pltpu.VMEM((tile_rows, SUB + 1, SUB, 128), jnp.float32),
                pltpu.SemaphoreType.DMA((4 * tile_rows + 1,)),
                pltpu.SemaphoreType.DMA((2 * tile_rows,)),
            ],
            flops=60 * tile_rows * tile_order * rank_cap * rank_cap,
        )
        return (
            new_basis.reshape(tile_rows * tile_order, rank_cap),
            new_factor.reshape(tile_rows * tile_order, rank_cap),
        )

    return shards


def solution(mesh):
    return jax.shard_map(
        make_shards(mesh.shape["row"], mesh.shape["col"]),
        mesh=mesh,
        in_specs=(
            P(("row", "col"), None),
            P(("row", "col"), None),
            P(("row", "col"), None),
            P("row"),
            P("row", "col"),
            P("row", "col"),
            P("row", "col"),
            P("row", "col"),
        ),
        out_specs=(P("row", "col"), P("row", "col")),
        check_vma=False,
    )
```
